512 devices in a mesh: gx: 8 (over y, core), gy: 16 (over z), grp: 4 (over x).
Axes of the slice: x: 4, y: 4, z: 16, core: 2. Of those that a mesh axis runs over, the one named last changes fastest.
Arguments:
- rhs: bfloat16 [4096, 64, 128], P(('gx', 'gy', 'grp')), may hold values from -6 to 6
- element_blocks: float32 [4096, 64, 448], P(('gx', 'gy', 'grp')), may hold values from -2 to 16
- element_table: int32 [4096, 6], P(('gx', 'gy', 'grp')), may hold values from -1 to 23, as said below
- element_block_inverses: float32 [4096, 64, 64], P(('gx', 'gy', 'grp')), may hold values from -1 to 2
- basis: float32 [4096, 64, 8], P(('gx', 'gy', 'grp')), may hold values from -0.75 to 0.75
- element_aggregate: int32 [4096], P(('gx', 'gy', 'grp')), may hold values from 0 to 1, as said below
- aggregate_blocks: float32 [1024, 8, 56], P(('gx', 'gy', 'grp')), may hold values from -2 to 16
- aggregate_table: int32 [1024, 6], P(('gx', 'gy', 'grp')), may hold values from -1 to 5, as said below
- aggregate_inverse: float32 [1024, 8, 8], P(('gx', 'gy', 'grp')), may hold values from -1 to 2
- coarse_map: int32 [1024], P(('gx', 'gy', 'grp')), may hold values from 0 to 7, as said below
- coarse_owner: int32 [128, 8], P(('gx', 'gy')), may hold values from 0 to 3, as said below
- coarse_inverse: float32 [128, 64, 64], P(('gx', 'gy')), may hold values from -1 to 2
Outputs:
- solution: float32 [4096, 64, 128], P(('gx', 'gy', 'grp'))
- new_residual: float32 [4096, 64, 128], P(('gx', 'gy', 'grp'))
The draws below stay inside these ranges and needn't reach their ends.
Inputs may be any that keep to these rules, and one draw needn't show every extreme that they name: `element_table`: row e of a device lists its neighbours across the faces -x, +x, -y, +y, -z, +z. A value t below 8 names element t of the previous device along gx+gy+grp, one below 16 element t - 8 of the same device, one from 16 on element t - 16 of the next device, and -1 no neighbour. Only column 0 names the previous device and only column 1 the next; on every device that has a previous one, exactly 4 of its rows name it, all different elements, and likewise for the next one. Neighbourhood is mutual. `element_aggregate`: each aggregate of a device holds 4 of its elements. `aggregate_table`: as for element_table, with 2 in place of 8 and 2 rows naming each neighbouring device. `coarse_map`: each of the 8 coarsest aggregates of a group gathers exactly 1 aggregate. `coarse_owner`: in every group one device owns exactly 4 coarsest aggregates and none owns more.
All inputs are finite; a program needn't handle non-finite values.
Results may differ from the reference program's by a relative error of at most 0.0003.
Values sent between devices are 32-bit elements; how exact they have to be, the bound alone decides.
A program may use at most 64 MiB of HBM per device.

```python
import jax
import jax.numpy as jnp
from jax import lax

NODES = 64
MODES = 8
LOADS = 128
XLAYERS = 2
YCELLS = 2
ZCELLS = 2
ELEMS = 8
AGGS = 2
ELEMS_ALL = 4096
AGGS_ALL = 1024
GROUPS = 128
COARSE = 8
COARSE_MOST = 4
COARSE_ROWS = 64
N_GX = 8
N_GY = 16
N_GRP = 4


def layer_perms(base_key, number, first_layer):
    devices = N_GX * N_GY * N_GRP

    def single(device):
        subkey = jax.random.fold_in(base_key, device)
        ordering = jax.random.permutation(jax.random.fold_in(subkey, 1), number).astype(jnp.int32)
        chosen = jax.random.randint(jax.random.fold_in(subkey, 2), (), 0, first_layer, dtype=jnp.int32)
        where_at = jnp.argmax(ordering == chosen)
        ordering = ordering.at[where_at].set(ordering[number - 1])
        return ordering.at[number - 1].set(chosen)
    return jax.vmap(single)(jnp.arange(devices, dtype=jnp.int32))


def build_table(ordering, depth, height, breadth):
    devices, number = ordering.shape
    layer_size = height * breadth
    slot_of = jnp.argsort(ordering, axis=1).astype(jnp.int32)
    xcoord = ordering // layer_size
    ycoord = ordering // breadth % height
    zcoord = ordering % breadth
    device_ids = jnp.arange(devices, dtype=jnp.int32)[:, None]
    prior_slots = jnp.roll(slot_of, 1, axis=0)
    later_slots = jnp.roll(slot_of, -1, axis=0)

    def lookup(source, target):
        return jnp.take_along_axis(source, jnp.clip(target, 0, number - 1), axis=1)
    minus_x = jnp.where(xcoord > 0, number + lookup(slot_of, ordering - layer_size), jnp.where(device_ids > 0, lookup(prior_slots, ordering + (depth - 1) * layer_size), -1))
    plus_x = jnp.where(xcoord < depth - 1, number + lookup(slot_of, ordering + layer_size), jnp.where(device_ids < devices - 1, 2 * number + lookup(later_slots, ordering - (depth - 1) * layer_size), -1))

    def within(row_index, depth_index):
        return number + lookup(slot_of, (xcoord * height + row_index) * breadth + depth_index)
    minus_y = within((ycoord + height - 1) % height, zcoord)
    plus_y = within((ycoord + 1) % height, zcoord)
    minus_z = within(ycoord, (zcoord + breadth - 1) % breadth)
    plus_z = within(ycoord, (zcoord + 1) % breadth)
    table = jnp.stack([minus_x, plus_x, minus_y, plus_y, minus_z, plus_z], axis=-1)
    return table.reshape(devices * number, 6).astype(jnp.int32)


def element_ordering(key):
    return layer_perms(jax.random.fold_in(key, 11), ELEMS, YCELLS * ZCELLS)


def aggregate_ordering(key):
    return layer_perms(jax.random.fold_in(key, 12), AGGS, YCELLS // 2 * ZCELLS)


def row_scales(key, number, salt, top):
    values = jax.random.uniform(jax.random.fold_in(key, salt), (number,), jnp.float32)
    return jnp.exp(values * jnp.log(top))


def neighbour_factor(table, scales, per_device):
    total_rows = table.shape[0]
    rows = jnp.arange(total_rows, dtype=jnp.int32)
    start = rows // per_device * per_device - per_device
    neighbour = jnp.where(table >= 0, start[:, None] + table, rows[:, None])
    every_scale = jnp.concatenate([scales[:, None], scales[neighbour]], axis=1)
    return jnp.sqrt(scales[:, None] * every_scale)


def operator_block_matrices(key, factor, total_rows, breadth):
    own_bound = 0.12 / (breadth - 1)
    side_bound = 0.1 / (6 * breadth)
    own_noise = jax.random.uniform(jax.random.fold_in(key, 1), (total_rows, breadth, breadth), jnp.float32, -own_bound, own_bound)
    side_noise = jax.random.uniform(jax.random.fold_in(key, 2), (total_rows, 6, breadth, breadth), jnp.float32, -side_bound, side_bound)
    coupling = jax.random.uniform(jax.random.fold_in(key, 3), (total_rows, 6), jnp.float32, 0.06, 0.12)
    identity = jnp.eye(breadth, dtype=jnp.float32)
    own_block = identity + own_noise * (1.0 - identity)
    side_blocks = side_noise - coupling[:, :, None, None] * identity
    blocks = jnp.concatenate([own_block[:, None], side_blocks], axis=1)
    blocks = blocks * factor[:, :, None, None]
    return jnp.transpose(blocks, (0, 2, 1, 3)).reshape(total_rows, breadth, 7 * breadth)


def inverse_blocks(key, scales, total_rows, breadth):
    bound = 0.5 / breadth
    noise = jax.random.uniform(key, (total_rows, breadth, breadth), jnp.float32, -bound, bound)
    identity = jnp.eye(breadth, dtype=jnp.float32)
    return (identity + noise * (1.0 - identity)) / scales[:, None, None]


def draw_element_table(key, part):
    ordering = element_ordering(key)
    return build_table(ordering, XLAYERS, YCELLS, ZCELLS)


def draw_element_aggregate(key, part):
    ordering = element_ordering(key)
    grouping = aggregate_ordering(key)
    layer_size = YCELLS * ZCELLS
    xcoord = ordering // layer_size
    ycoord = ordering // ZCELLS % YCELLS
    zcoord = ordering % ZCELLS
    natural = (xcoord // 2 * (YCELLS // 2) + ycoord // 2) * ZCELLS + zcoord
    slot_of = jnp.argsort(grouping, axis=1).astype(jnp.int32)
    return jnp.take_along_axis(slot_of, natural, axis=1).reshape(-1).astype(jnp.int32)


def draw_aggregate_table(key, part):
    grouping = aggregate_ordering(key)
    return build_table(grouping, XLAYERS // 2, YCELLS // 2, ZCELLS)


def draw_element_blocks(key, part):
    top = 10.0
    scales = row_scales(key, ELEMS_ALL, 13, top)
    table = build_table(element_ordering(key), XLAYERS, YCELLS, ZCELLS)
    key = jax.random.fold_in(key, 4)
    factor = neighbour_factor(table, scales, ELEMS)
    return operator_block_matrices(key, factor, ELEMS_ALL, NODES).astype(jnp.float32)


def draw_element_block_inverses(key, part):
    top = 10.0
    scales = row_scales(key, ELEMS_ALL, 13, top)
    key = jax.random.fold_in(key, 5)
    return inverse_blocks(key, scales, ELEMS_ALL, NODES).astype(jnp.float32)


def draw_aggregate_blocks(key, part):
    top = 10.0
    scales = row_scales(key, AGGS_ALL, 14, top)
    table = build_table(aggregate_ordering(key), XLAYERS // 2, YCELLS // 2, ZCELLS)
    key = jax.random.fold_in(key, 6)
    factor = neighbour_factor(table, scales, AGGS)
    return operator_block_matrices(key, factor, AGGS_ALL, MODES).astype(jnp.float32)


def draw_aggregate_inverse(key, part):
    top = 10.0
    scales = row_scales(key, AGGS_ALL, 14, top)
    key = jax.random.fold_in(key, 7)
    return inverse_blocks(key, scales, AGGS_ALL, MODES).astype(jnp.float32)


def draw_coarse_map(key, part):
    key = jax.random.fold_in(key, 8)

    def single(group):
        ordering = jax.random.permutation(jax.random.fold_in(key, group), N_GRP * AGGS).astype(jnp.int32)
        return ordering % COARSE
    groups = N_GX * N_GY
    return jax.vmap(single)(jnp.arange(groups, dtype=jnp.int32)).reshape(-1).astype(jnp.int32)


def draw_coarse_owner(key, part):
    key = jax.random.fold_in(key, 9)

    def single(group):
        subkey = jax.random.fold_in(key, group)
        busiest = jax.random.randint(jax.random.fold_in(subkey, 1), (), 0, N_GRP, dtype=jnp.int32)
        extra = jax.random.randint(jax.random.fold_in(subkey, 2), (1,), 0, N_GRP - 1, dtype=jnp.int32)
        others = (busiest + 1 + jnp.concatenate([jnp.arange(N_GRP - 1, dtype=jnp.int32), extra])) % N_GRP
        owners = jnp.concatenate([jnp.full((COARSE_MOST,), busiest, jnp.int32), others])
        ordering = jax.random.permutation(jax.random.fold_in(subkey, 3), COARSE)
        return owners[ordering]
    groups = N_GX * N_GY
    return jax.vmap(single)(jnp.arange(groups, dtype=jnp.int32)).astype(jnp.int32)


def draw_coarse_inverse(key, part):
    key = jax.random.fold_in(key, 10)
    groups = N_GX * N_GY
    diagonal = 1.0 + jax.random.uniform(jax.random.fold_in(key, 1), (groups, COARSE_ROWS), jnp.float32)
    bound = 1.0 / COARSE_ROWS
    noise = jax.random.uniform(jax.random.fold_in(key, 2), (groups, COARSE_ROWS, COARSE_ROWS), jnp.float32, -bound, bound)
    identity = jnp.eye(COARSE_ROWS, dtype=jnp.float32)
    return noise * (1.0 - identity) + identity * diagonal[:, :, None]


def levels(own_key, shape, split, least, largest):
    factor_of = 1.0
    for axis_at, parts in split:
        heights = jax.random.uniform(jax.random.fold_in(jax.random.fold_in(own_key, 6), axis_at), (parts,), jnp.float32, least / len(split), largest / len(split))
        factor_of = factor_of * jnp.repeat(jnp.exp(heights), shape[axis_at] // parts).reshape((-1,) + (1,) * (len(shape) - 1 - axis_at))
    return factor_of


def scatter_about(stream_key, shape, width, most, cuts=(), kind=jnp.bfloat16):
    drawn = width * jax.random.normal(stream_key, shape, jnp.float32)
    if cuts:
        drawn = drawn * levels(stream_key, shape, cuts, -0.22, 0.18)
    return jnp.clip(drawn, -most, most).astype(kind)


def setup_inputs(seed: int = 0) -> dict:
    key_list = jax.random.split(jax.random.key(seed), 13)
    rhs = scatter_about(key_list[0], (ELEMS_ALL, NODES, LOADS), 1.0, 6.0, ((0, 512),))
    element_blocks = draw_element_blocks(jax.random.fold_in(key_list[12], 71), 0)
    element_table = draw_element_table(jax.random.fold_in(key_list[12], 71), 0)
    element_block_inverses = draw_element_block_inverses(jax.random.fold_in(key_list[12], 71), 0)
    basis = scatter_about(key_list[4], (ELEMS_ALL, NODES, MODES), NODES ** -0.5, 0.75, ((0, 512),), jnp.float32)
    element_aggregate = draw_element_aggregate(jax.random.fold_in(key_list[12], 71), 0)
    aggregate_blocks = draw_aggregate_blocks(jax.random.fold_in(key_list[12], 71), 0)
    aggregate_table = draw_aggregate_table(jax.random.fold_in(key_list[12], 71), 0)
    aggregate_inverse = draw_aggregate_inverse(jax.random.fold_in(key_list[12], 71), 0)
    coarse_map = draw_coarse_map(jax.random.fold_in(key_list[12], 71), 0)
    coarse_owner = draw_coarse_owner(jax.random.fold_in(key_list[12], 71), 0)
    coarse_inverse = draw_coarse_inverse(jax.random.fold_in(key_list[12], 71), 0)
    return dict(rhs=rhs, element_blocks=element_blocks, element_table=element_table, element_block_inverses=element_block_inverses, basis=basis, element_aggregate=element_aggregate, aggregate_blocks=aggregate_blocks, aggregate_table=aggregate_table, aggregate_inverse=aggregate_inverse, coarse_map=coarse_map, coarse_owner=coarse_owner, coarse_inverse=coarse_inverse)


OMEGA = 0.7
LOW_BOUND = 0.25
UPPER_LIMIT = 1.9
TOP_PRECISION = lax.Precision.HIGHEST


def block_product(blocks, neighbours, vector, per_device):
    total_rows, block_width, columns = vector.shape
    devices = total_rows // per_device
    shaped = vector.reshape(devices, per_device, block_width, columns)
    edge_slab = jnp.zeros((1, per_device, block_width, columns), jnp.float32)
    padded = jnp.concatenate([edge_slab, shaped, edge_slab], axis=0)
    tables = neighbours.reshape(devices, per_device, 6)
    matrices = blocks.reshape(devices, per_device, block_width, 7 * block_width)
    blank_row = jnp.zeros((1, block_width, columns), jnp.float32)

    def per_slab(device):
        window = lax.dynamic_slice_in_dim(padded, device, 3, 0).reshape(3 * per_device, block_width, columns)
        window = jnp.concatenate([window, blank_row], axis=0)
        local_rows = tables[device]
        picked = jnp.where(local_rows < 0, 3 * per_device, local_rows)
        gathered = window[picked]
        stacked = jnp.concatenate([shaped[device][:, None], gathered], axis=1)
        stacked = stacked.reshape(per_device, 7 * block_width, columns)
        return jnp.einsum("eij,ejr->eir", matrices[device], stacked, precision=TOP_PRECISION)

    result = lax.map(per_slab, jnp.arange(devices, dtype=jnp.int32))
    return result.reshape(total_rows, block_width, columns)


def inverse_product(inverses, vector):
    return jnp.einsum("eij,ejr->eir", inverses, vector, precision=TOP_PRECISION)


def chebyshev(apply_matrix, apply_inverse, right, start):
    theta = (UPPER_LIMIT + LOW_BOUND) / 2.0
    delta = (UPPER_LIMIT - LOW_BOUND) / 2.0
    sigma = theta / delta
    rho = 1.0 / sigma
    if start is None:
        update = apply_inverse(right)
        answer = jnp.zeros_like(right)
    else:
        update = apply_inverse(right - apply_matrix(start))
        answer = start
    direction = update / theta
    answer = answer + direction
    for repeat_step in range(2):
        update = update - apply_inverse(apply_matrix(direction))
        rho_next = 1.0 / (2.0 * sigma - rho)
        direction = (rho_next * rho) * direction + (2.0 * rho_next / delta) * update
        answer = answer + direction
        rho = rho_next
    return answer


def reference(rhs, element_blocks, element_table, element_block_inverses, basis, element_aggregate, aggregate_blocks, aggregate_table, aggregate_inverse, coarse_map, coarse_owner, coarse_inverse):
    def fine_matrix(vector):
        return block_product(element_blocks, element_table, vector, ELEMS)

    def fine_inverse(vector):
        return inverse_product(element_block_inverses, vector)

    def middle_matrix(vector):
        return block_product(aggregate_blocks, aggregate_table, vector, AGGS)

    def middle_inverse(vector):
        return inverse_product(aggregate_inverse, vector)

    residual = rhs.astype(jnp.float32)
    presmooth = chebyshev(fine_matrix, fine_inverse, residual, None)
    defect = residual - fine_matrix(presmooth)
    smoothed = defect - OMEGA * fine_matrix(fine_inverse(defect))
    owner_of = (jnp.arange(ELEMS_ALL, dtype=jnp.int32) // ELEMS) * AGGS + element_aggregate.astype(jnp.int32)
    projected = jnp.einsum("epk,epr->ekr", basis, smoothed, precision=TOP_PRECISION)
    residual_one = jax.ops.segment_sum(projected, owner_of, num_segments=AGGS_ALL)
    pre_one = chebyshev(middle_matrix, middle_inverse, residual_one, None)
    defect_one = residual_one - middle_matrix(pre_one)
    group_of = jnp.arange(AGGS_ALL, dtype=jnp.int32) // (N_GRP * AGGS)
    segment_ids = group_of * COARSE + coarse_map.astype(jnp.int32)
    coarse_right_side = jax.ops.segment_sum(defect_one, segment_ids, num_segments=GROUPS * COARSE)
    coarse_right_side = coarse_right_side.reshape(GROUPS, COARSE_ROWS, LOADS)
    owner_rows = jnp.repeat(coarse_owner, MODES, axis=1)
    masked_values = jnp.where(owner_rows[:, :, None] == owner_rows[:, None, :], coarse_inverse, jnp.zeros_like(coarse_inverse))
    coarse_answer_vector = jnp.einsum("kax,kxz->kaz", masked_values, coarse_right_side, precision=TOP_PRECISION)
    coarse_answer_vector = coarse_answer_vector.reshape(GROUPS * COARSE, MODES, LOADS)
    post_one = chebyshev(middle_matrix, middle_inverse, residual_one, pre_one + coarse_answer_vector[segment_ids])
    spread_values = post_one[owner_of]
    lifted = jnp.einsum("epk,ekr->epr", basis, spread_values, precision=TOP_PRECISION)
    correction = lifted - OMEGA * fine_inverse(fine_matrix(lifted))
    precond = chebyshev(fine_matrix, fine_inverse, residual, presmooth + correction)
    numerator = jnp.sum(residual * precond, axis=(0, 1))
    applied = fine_matrix(precond)
    denominator = jnp.sum(precond * applied, axis=(0, 1))
    step_size = numerator / denominator
    return step_size * precond, residual - step_size * applied
```

```python
import functools

import jax
import jax.numpy as jnp
from jax import lax
from jax.experimental import pallas as pl
from jax.experimental.pallas import tpu as pltpu
from jax.sharding import PartitionSpec as P

OMEGA = 0.7
LOW_BOUND = 0.25
UPPER_LIMIT = 1.9
THETA = (UPPER_LIMIT + LOW_BOUND) / 2.0
DELTA = (UPPER_LIMIT - LOW_BOUND) / 2.0
SIGMA = THETA / DELTA
RHO = [1.0 / SIGMA]
for _ in range(2):
    RHO.append(1.0 / (2.0 * SIGMA - RHO[-1]))
KEEP = [0.0, RHO[1] * RHO[0], RHO[2] * RHO[1]]
TAKE = [1.0 / THETA, 2.0 * RHO[1] / DELTA, 2.0 * RHO[2] / DELTA]

ELEMS = 8
NODES = 64
MODES = 8
LOADS = 128
HALO = 4
REACH = 2
SPAN = 2 * REACH + 1
MESH = pl.DeviceIdType.MESH
HIGHEST = lax.Precision.HIGHEST
F32 = jnp.float32
BF16 = jnp.bfloat16


def dot(a, b):
    return jnp.dot(a, b, preferred_element_type=F32)


def exact(a, b):
    return jnp.dot(a, b, preferred_element_type=F32, precision=HIGHEST)


def three(v):
    high = v.astype(BF16)
    rest = v - high.astype(F32)
    middle = rest.astype(BF16)
    low = (rest - middle.astype(F32)).astype(BF16)
    return high, middle, low


def iota(shape, dim):
    return lax.broadcasted_iota(jnp.int32, shape, dim)


def kernel(
    sizes,
    table,
    member,
    coarse_table,
    coarse_map,
    owner,
    rhs,
    blocks,
    inverses,
    basis,
    coarse_blocks,
    coarse_inverses,
    group_inverse,
    x_out,
    applied_out,
    step_out,
    near,
    far,
    give,
    da,
    a,
    window,
    halo,
    update,
    direction,
    answer,
    acc,
    field,
    sent,
    landed,
    prolong,
    prolong_t,
    prolong_sent,
    prolong_landed,
    pack,
    packs,
    level,
    kmat,
    amat,
    cmat,
    dmat,
    strip,
    own_b,
    all_b,
    part,
    parts_near,
    total,
    parts_far,
    send_sem,
    recv_sem,
    pro_send,
    pro_recv,
    pack_send,
    pack_recv,
    b_send,
    b_recv,
    sum_send,
    sum_recv,
):
    ngx, ngy, ngrp = sizes
    groups = ngx * ngy
    devices = groups * ngrp
    wide = SPAN * ngrp * 16
    full = level.shape[0]
    gx, gy, grp = (lax.axis_index(name) for name in ("gx", "gy", "grp"))
    group = gx * ngy + gy
    me = group * ngrp + grp

    def place(index):
        return (index // (ngy * ngrp), (index // ngrp) % ngy, index % ngrp)

    before = place((me + devices - 1) % devices)
    after = place((me + 1) % devices)

    def gather_partner(i):
        offset = i // ngrp
        offset = jnp.where(offset > REACH, offset - SPAN, offset)
        to_group = (group + offset + groups) % groups
        to_grp = (grp + i) % ngrp
        slot = (REACH - offset) * ngrp + grp
        return (to_group // ngy, to_group % ngy, to_grp), slot

    near_count = ngx * ngrp
    near_rank = gx * ngrp + grp

    def near_partner(i):
        rank = (near_rank + i) % near_count
        return (rank // ngrp, gy, rank % ngrp)

    def far_partner(i):
        return (gx, (gy + i) % ngy, grp)

    barrier = pltpu.get_barrier_semaphore()

    def greet(partner, count):
        def body(i, carry):
            pl.semaphore_signal(barrier, inc=1, device_id=partner(i), device_id_type=MESH)
            return carry

        lax.fori_loop(1, count, body, 0)

    greet(lambda i: gather_partner(i)[0], SPAN * ngrp)
    greet(near_partner, near_count)
    greet(far_partner, ngy)
    greetings = (SPAN * ngrp - 1) + (near_count - 1) + (ngy - 1)

    for e in range(ELEMS):
        for k in range(6):
            t = table[e, k]
            here = (t >= ELEMS) & (t < 2 * ELEMS)
            near[e, k] = jnp.where(here, t - ELEMS, ELEMS)
        low, high = table[e, 0], table[e, 1]
        low_rank = jnp.int32(0)
        high_rank = jnp.int32(0)
        for other in range(ELEMS):
            t = table[other, 0]
            low_rank += ((t >= 0) & (t < low)).astype(jnp.int32)
            t = table[other, 1]
            high_rank += ((t >= 2 * ELEMS) & (t < high)).astype(jnp.int32)
        named = (low >= 0) & (low < ELEMS)
        far[e, 0] = jnp.where(named, jnp.minimum(low_rank, HALO - 1), 2 * HALO)
        far[e, 1] = jnp.where(high >= 2 * ELEMS, HALO + jnp.minimum(high_rank, HALO - 1), 2 * HALO)
    for side in range(2):
        chosen = [jnp.int32(0) for _ in range(HALO)]
        count = jnp.int32(0)
        for e in range(ELEMS):
            t = table[e, side]
            flag = (t >= 0) & (t < ELEMS) if side == 0 else t >= 2 * ELEMS
            chosen = [jnp.where(flag & (count == j), e, chosen[j]) for j in range(HALO)]
            count += flag.astype(jnp.int32)
        for j in range(HALO):
            give[side, j] = chosen[j]

    window[ELEMS] = jnp.zeros((NODES, 3 * LOADS), BF16)
    halo[2 * HALO] = jnp.zeros((NODES, 3 * LOADS), BF16)

    for e in range(ELEMS):
        spot = iota((MODES, LOADS), 1) == iota((MODES, LOADS), 0) + MODES * member[e]
        prolong[e] = exact(basis[e], spot.astype(F32))
    for side in range(2):
        prolong_sent[side] = sum(
            pltpu.roll(prolong[give[side, j]], 16 * j, 1) if j else prolong[give[side, j]]
            for j in range(HALO)
        )

    lanes = iota((8, 128), 1)
    for agg in range(2):
        row = iota((56, 128), 0)
        want = jnp.full((56, 128), 2 + agg, jnp.int32)
        for k in range(6):
            want = jnp.where(row // 8 == k + 1, coarse_table[agg, k], want)
        spot = iota((56, 128), 1) == want * 8 + row % 8
        t_rows = exact(coarse_blocks[agg], spot.astype(F32))
        small = iota((8, 128), 1) == iota((8, 128), 0) + 48 + 8 * agg
        d_rows = exact(coarse_inverses[agg], small.astype(F32))
        whole = coarse_map[agg]
        coarse_rows = group_inverse[whole]
        mine = owner[0, whole]
        kept = jnp.zeros((8, 64), F32)
        for c in range(8):
            same = (owner[0, c] == mine).astype(F32)
            kept = jnp.where(iota((8, 64), 1) // 8 == c, same, kept)
        shift = iota((64, 128), 1) == iota((64, 128), 0) + 64
        m_rows = exact(jnp.where(kept > 0.5, coarse_rows, 0.0), shift.astype(F32))
        s_rows = (lanes == iota((8, 128), 0) + 8 * whole).astype(F32)
        dt_rows = pltpu.roll(exact(coarse_inverses[agg], t_rows), 64, 1)
        first = jnp.where(lanes < 48, t_rows, jnp.where(lanes < 64, d_rows, m_rows))
        pack[8 * agg : 8 * agg + 8, 0:128] = first
        pack[8 * agg : 8 * agg + 8, 128:256] = jnp.where(lanes < 64, s_rows, dt_rows)

    for e in range(ELEMS):
        pieces = jnp.concatenate(three(inverses[e]), axis=0)
        o = dot(pieces, rhs[e])
        q = o[0:64] + (o[64:128] + o[128:192])
        update[e] = q
        d = q * TAKE[0]
        direction[e] = d
        answer[e] = d

    pl.semaphore_wait(barrier, greetings)

    def ring(source, target, send, recv, side):
        return pltpu.make_async_remote_copy(
            src_ref=source,
            dst_ref=target,
            send_sem=send,
            recv_sem=recv,
            device_id=before if side == 0 else after,
            device_id_type=MESH,
        )

    pending = []

    def exchange(k, source):
        copies = []
        for side in range(2):
            for j in range(HALO):
                sent[k, side, j] = source[give[side, j]]
            copy = ring(
                sent.at[k, side], landed.at[k, 1 - side], send_sem.at[k, side], recv_sem.at[k, side], side
            )
            copy.start()
            copies.append(copy)
            pending.append(copy)
        return copies

    def cut(source):
        for e in range(ELEMS):
            high, middle, low = three(source[e])
            window[e, :, 0:128] = high
            window[e, :, 128:256] = middle
            window[e, :, 256:384] = low

    def cut_halo(source, slot):
        high, middle, low = three(source)
        halo[slot, :, 0:128] = high
        halo[slot, :, 128:256] = middle
        halo[slot, :, 256:384] = low

    def products(matrix, stack):
        o = dot(matrix, stack[:, 0:256])
        p = dot(matrix[0:64], stack[:, 256:384])
        small = o[64:128, 128:256] + o[128:192, 0:128] + p
        return o[0:64, 0:128] + ((o[0:64, 128:256] + o[64:128, 0:128]) + small)

    def local_part(matrix, e):
        stack = jnp.concatenate([window[e]] + [window[near[e, k]] for k in range(6)], axis=0)
        return products(matrix[e], stack)

    def halo_part(matrix, e):
        stack = jnp.concatenate([halo[far[e, 0]], halo[far[e, 1]]], axis=0)
        return products(matrix[e, :, 64:192], stack)

    def apply(k, matrix, source, finish, between=None):
        copies = exchange(k, source)
        cut(source)
        for e in range(ELEMS):
            acc[e] = local_part(matrix, e)
        if between is not None:
            between()
        for copy in copies:
            copy.wait_recv()
        for side in range(2):
            for j in range(HALO):
                cut_halo(landed[k, side, j], side * HALO + j)
        for e in range(ELEMS):
            finish(e, acc[e] + halo_part(matrix, e))

    def prepare():
        for e in range(ELEMS):
            high, middle, low = three(blocks[e])
            a[e, 0:64] = high
            a[e, 64:128] = middle
            a[e, 128:192] = low
            high, middle, low = three(exact(inverses[e], blocks[e]))
            da[e, 0:64] = high
            da[e, 64:128] = middle
            da[e, 128:192] = low

    for side in range(2):
        copy = ring(
            prolong_sent.at[side], prolong_landed.at[1 - side], pro_send.at[side], pro_recv.at[side], side
        )
        copy.start()
        pending.append(copy)

    def gather(source, target, send, recv):
        own_slot = REACH * ngrp + grp

        def body(i, carry):
            device, slot = gather_partner(i)
            pltpu.make_async_remote_copy(
                src_ref=source,
                dst_ref=target.at[slot],
                send_sem=send,
                recv_sem=recv,
                device_id=device,
                device_id_type=MESH,
            ).start()
            return carry

        lax.fori_loop(1, SPAN * ngrp, body, 0)
        target[own_slot] = source[...]

    def wait_bytes(target, count, sem):
        pltpu.make_async_copy(target.at[pl.ds(0, count)], target.at[pl.ds(0, count)], sem).wait()

    gathered = SPAN * ngrp - 1

    def level_matrices():
        wait_bytes(packs, gathered, pack_recv)
        wait_bytes(packs, gathered, pack_send)
        rows_of = SPAN * ngrp
        for ref in (kmat, amat, cmat, dmat):
            ref[...] = jnp.zeros((full, full), F32)
        blank = jnp.zeros((16, full - 128), F32)

        def spread(rows, first, count, move):
            keep = (iota((16, 128), 1) >= first) & (iota((16, 128), 1) < first + count)
            rows = jnp.concatenate([jnp.where(keep, rows, 0.0), blank], axis=1)
            return pltpu.roll(rows, (move - first) % full, 1)

        for w in range(rows_of):
            one = packs[w, :, 0:128]
            two = packs[w, :, 128:256]
            here = slice(16 * w, 16 * w + 16)
            amat[here, :] = spread(one, 0, 48, 16 * (w - 1))
            dmat[here, :] = spread(one, 48, 16, 16 * w)
            kmat[here, :] = spread(two, 64, 48, 16 * (w - 1))
        for s in range(SPAN):
            parts = [packs[s * ngrp + j] for j in range(ngrp)]
            stacked = jnp.concatenate(parts, axis=0)
            coarse = stacked[:, 64:128]
            places = stacked[:, 128:192]
            block = lax.dot_general(
                coarse, places, (((1,), (1,)), ((), ())), preferred_element_type=F32, precision=HIGHEST
            )
            size = 16 * ngrp
            row = jnp.concatenate([block, jnp.zeros((size, full - size), F32)], axis=1)
            cmat[size * s : size * s + size, :] = pltpu.roll(row, size * s, 1) if s else row

    def smooth(rows):
        q = rows
        d = rows * TAKE[0]
        y = d
        for i in (1, 2):
            q = q - exact(d, kmat[...])
            d = KEEP[i] * d + TAKE[i] * q
            y = y + d
        return y

    def level_strip():
        first = (REACH * ngrp + grp - 1) * 16
        unit = (iota((48, full), 1) == iota((48, full), 0) + first).astype(F32)
        u = smooth(unit)
        v = exact(u, kmat[...])
        m = exact(unit - v, cmat[...])
        y = smooth(v + exact(m, amat[...]))
        strip[...] = m + exact(2.0 * u - y, dmat[...])

    def pre_finish(i):
        def finish(e, value):
            q = update[e] - value
            update[e] = q
            if i < 3:
                d = KEEP[i] * direction[e] + TAKE[i] * q
                direction[e] = d
                answer[e] = answer[e] + d
            else:
                field[e] = answer[e] + OMEGA * q

        return finish

    def first_between():
        gather(pack, packs, pack_send, pack_recv)

    copies = exchange(0, direction)
    gather(pack, packs, pack_send, pack_recv)
    prepare()
    cut(direction)
    for e in range(ELEMS):
        acc[e] = local_part(da, e)
    for copy in copies:
        copy.wait_recv()
    for side in range(2):
        for j in range(HALO):
            cut_halo(landed[0, side, j], side * HALO + j)
    for e in range(ELEMS):
        pre_finish(1)(e, acc[e] + halo_part(da, e))
    apply(1, da, direction, pre_finish(2), level_matrices)
    apply(2, da, direction, pre_finish(3), level_strip)

    big = jnp.concatenate([prolong[e] for e in range(ELEMS)], axis=0)
    prolong_t[...] = big.T[0:16]

    def restrict(e, value):
        acc[e] = rhs[e].astype(F32) - value

    apply(3, a, field, restrict)
    own_b[...] = exact(prolong_t[...], acc[...].reshape(ELEMS * NODES, LOADS))

    gather(own_b, all_b, b_send, b_recv)
    wait_bytes(all_b, gathered, b_recv)
    wait_bytes(all_b, gathered, b_send)
    values = all_b[...].reshape(wide, LOADS)
    padded = jnp.concatenate([values, jnp.zeros((full - wide, LOADS), F32)], axis=0)
    c = exact(strip[...], padded)

    blank = jnp.zeros((128 - 16, LOADS), F32)
    own_c = jnp.concatenate([c[16:32], blank], axis=0)
    for e in range(ELEMS):
        field[e] = exact(prolong[e], own_c)
    cut(field)
    pro = pending[2:4]
    for copy in (pro if False else []):
        copy.wait_recv()
    for side in range(2):
        ring(
            prolong_sent.at[side], prolong_landed.at[1 - side], pro_send.at[side], pro_recv.at[side], side
        ).wait_recv()
    for side in range(2):
        rows = c[0:16] if side == 0 else c[32:48]
        for j in range(HALO):
            above = [jnp.zeros((16 * j, LOADS), F32)] if j else []
            spot = jnp.concatenate(above + [rows, jnp.zeros((112 - 16 * j, LOADS), F32)], axis=0)
            cut_halo(exact(prolong_landed[side], spot), side * HALO + j)
    for e in range(ELEMS):
        w = local_part(da, e) + halo_part(da, e)
        direction[e] = w
        update[e] = update[e] - w
        answer[e] = answer[e] + field[e] - OMEGA * w

    def post_finish(i):
        def finish(e, value):
            if i == 0:
                q = update[e] + OMEGA * value
                d = TAKE[0] * q
            else:
                q = update[e] - value
                d = KEEP[i] * direction[e] + TAKE[i] * q
            update[e] = q
            direction[e] = d
            answer[e] = answer[e] + d

        return finish

    apply(4, da, direction, post_finish(0))
    apply(5, da, direction, post_finish(1))
    apply(6, da, direction, post_finish(2))

    sums = [jnp.zeros((8, LOADS), F32), jnp.zeros((8, LOADS), F32)]

    def last(e, value):
        x = answer[e]
        applied_out[e] = value
        x_out[e] = x
        r = rhs[e].astype(F32)
        sums[0] = sums[0] + jnp.sum((r * x).reshape(8, 8, LOADS), axis=0)
        sums[1] = sums[1] + jnp.sum((x * value).reshape(8, 8, LOADS), axis=0)

    apply(7, a, answer, last)
    row = iota((8, LOADS), 0)
    numerator = jnp.sum(sums[0], axis=0, keepdims=True)
    denominator = jnp.sum(sums[1], axis=0, keepdims=True)
    part[...] = jnp.where(row == 0, numerator, jnp.where(row == 1, denominator, 0.0))

    def combine(source, target, partner, rank, count, which):
        def body(i, carry):
            pltpu.make_async_remote_copy(
                src_ref=source,
                dst_ref=target.at[rank],
                send_sem=sum_send.at[which],
                recv_sem=sum_recv.at[which],
                device_id=partner(i),
                device_id_type=MESH,
            ).start()
            return carry

        lax.fori_loop(1, count, body, 0)
        target[rank] = source[...]
        wait_bytes(target, count - 1, sum_recv.at[which])
        wait_bytes(target, count - 1, sum_send.at[which])
        return jnp.sum(target[...], axis=0)

    total[...] = combine(part, parts_near, near_partner, near_rank, near_count, 0)
    whole = combine(total, parts_far, far_partner, gy, ngy, 1)
    step_out[...] = jnp.broadcast_to(whole[0:1] / whole[1:2], (8, LOADS))
    for copy in pending:
        copy.wait_send()


def on_device(
    sizes,
    rhs,
    element_blocks,
    element_table,
    element_block_inverses,
    basis,
    element_aggregate,
    aggregate_blocks,
    aggregate_table,
    aggregate_inverse,
    coarse_map,
    coarse_owner,
    coarse_inverse,
):
    ngx, ngy, ngrp = sizes
    held = SPAN * ngrp
    full = -(-held * 16 // 128) * 128
    smem = pl.BlockSpec(memory_space=pltpu.SMEM)
    vmem = pl.BlockSpec(memory_space=pltpu.VMEM)
    shape = (ELEMS, NODES, LOADS)
    exchanges = 8
    scratch = [
        pltpu.SMEM((ELEMS, 6), jnp.int32),
        pltpu.SMEM((ELEMS, 2), jnp.int32),
        pltpu.SMEM((2, HALO), jnp.int32),
        pltpu.VMEM((ELEMS, 192, 448), BF16),
        pltpu.VMEM((ELEMS, 192, 448), BF16),
        pltpu.VMEM((ELEMS + 1, NODES, 3 * LOADS), BF16),
        pltpu.VMEM((2 * HALO + 1, NODES, 3 * LOADS), BF16),
        pltpu.VMEM(shape, F32),
        pltpu.VMEM(shape, F32),
        pltpu.VMEM(shape, F32),
        pltpu.VMEM(shape, F32),
        pltpu.VMEM(shape, F32),
        pltpu.VMEM((exchanges, 2, HALO, NODES, LOADS), F32),
        pltpu.VMEM((exchanges, 2, HALO, NODES, LOADS), F32),
        pltpu.VMEM(shape, F32),
        pltpu.VMEM((16, ELEMS * NODES), F32),
        pltpu.VMEM((2, NODES, LOADS), F32),
        pltpu.VMEM((2, NODES, LOADS), F32),
        pltpu.VMEM((16, 256), F32),
        pltpu.VMEM((held, 16, 256), F32),
        pltpu.VMEM((full, full), F32),
        pltpu.VMEM((full, full), F32),
        pltpu.VMEM((full, full), F32),
        pltpu.VMEM((full, full), F32),
        pltpu.VMEM((full, full), F32),
        pltpu.VMEM((48, full), F32),
        pltpu.VMEM((16, LOADS), F32),
        pltpu.VMEM((held, 16, LOADS), F32),
        pltpu.VMEM((8, LOADS), F32),
        pltpu.VMEM((ngx * ngrp, 8, LOADS), F32),
        pltpu.VMEM((8, LOADS), F32),
        pltpu.VMEM((ngy, 8, LOADS), F32),
        pltpu.SemaphoreType.DMA((exchanges, 2)),
        pltpu.SemaphoreType.DMA((exchanges, 2)),
        pltpu.SemaphoreType.DMA((2,)),
        pltpu.SemaphoreType.DMA((2,)),
        pltpu.SemaphoreType.DMA,
        pltpu.SemaphoreType.DMA,
        pltpu.SemaphoreType.DMA,
        pltpu.SemaphoreType.DMA,
        pltpu.SemaphoreType.DMA((2,)),
        pltpu.SemaphoreType.DMA((2,)),
    ]
    x, applied, step = pl.pallas_call(
        functools.partial(kernel, sizes),
        out_shape=(
            jax.ShapeDtypeStruct(shape, F32),
            jax.ShapeDtypeStruct(shape, F32),
            jax.ShapeDtypeStruct((8, LOADS), F32),
        ),
        in_specs=[smem] * 5 + [vmem] * 7,
        out_specs=(vmem, vmem, vmem),
        scratch_shapes=scratch,
        compiler_params=pltpu.CompilerParams(
            collective_id=0, has_side_effects=True, vmem_limit_bytes=48 * 1024 * 1024
        ),
    )(
        element_table,
        element_aggregate,
        aggregate_table,
        coarse_map,
        coarse_owner,
        rhs,
        element_blocks,
        element_block_inverses,
        basis,
        aggregate_blocks,
        aggregate_inverse,
        coarse_inverse.reshape(8, 8, 64),
    )
    step = step[0:1][None]
    return step * x, rhs.astype(F32) - step * applied


def solution(mesh):
    sizes = tuple(mesh.shape[name] for name in ("gx", "gy", "grp"))
    slabs = P(("gx", "gy", "grp"), None, None)
    pairs = P(("gx", "gy", "grp"), None)
    ids = P(("gx", "gy", "grp"))
    return jax.shard_map(
        functools.partial(on_device, sizes),
        mesh=mesh,
        in_specs=(
            slabs,
            slabs,
            pairs,
            slabs,
            slabs,
            ids,
            slabs,
            pairs,
            slabs,
            ids,
            P(("gx", "gy"), None),
            P(("gx", "gy"), None, None),
        ),
        out_specs=(slabs, slabs),
        check_vma=False,
    )
```

```python
import functools

import jax
import jax.numpy as jnp
from jax import lax
from jax.experimental import pallas as pl
from jax.experimental.pallas import tpu as pltpu
from jax.sharding import PartitionSpec as P

OMEGA = 0.7
LOW_BOUND = 0.25
UPPER_LIMIT = 1.9
THETA = (UPPER_LIMIT + LOW_BOUND) / 2.0
DELTA = (UPPER_LIMIT - LOW_BOUND) / 2.0
SIGMA = THETA / DELTA
RHO = [1.0 / SIGMA]
for _ in range(2):
    RHO.append(1.0 / (2.0 * SIGMA - RHO[-1]))
KEEP = [0.0, RHO[1] * RHO[0], RHO[2] * RHO[1]]
TAKE = [1.0 / THETA, 2.0 * RHO[1] / DELTA, 2.0 * RHO[2] / DELTA]

ELEMS = 8
NODES = 64
MODES = 8
SIDE = 3
LOADS = 128
HALO = 4
REACH = 3
SPAN = 2 * REACH + 1
MESH = pl.DeviceIdType.MESH
HIGHEST = lax.Precision.HIGHEST
F32 = jnp.float32
BF16 = jnp.bfloat16


def dot(a, b):
    return jnp.dot(a, b, preferred_element_type=F32)


def exact(a, b):
    return jnp.dot(a, b, preferred_element_type=F32, precision=HIGHEST)


def three(v):
    high = v.astype(BF16)
    rest = v - high.astype(F32)
    middle = rest.astype(BF16)
    low = (rest - middle.astype(F32)).astype(BF16)
    return high, middle, low


def iota(shape, dim):
    return lax.broadcasted_iota(jnp.int32, shape, dim)


def kernel(
    sizes,
    table,
    member,
    coarse_table,
    coarse_map,
    owner,
    rhs_hbm,
    inverses_hbm,
    blocks_hbm,
    basis_hbm,
    coarse_blocks,
    coarse_inverses,
    group_inverse,
    x_out,
    applied_out,
    step_out,
    rhs,
    inverses,
    blocks,
    basis,
    near,
    far,
    give,
    edge,
    da,
    a,
    window,
    halo,
    window_m,
    halo_m,
    update,
    direction,
    answer,
    acc,
    field,
    sent,
    landed,
    prolong,
    prolong_t,
    m_one,
    m_two,
    m_three,
    m_sent,
    m_landed,
    strip_sent,
    strip_landed,
    share_sent,
    share_landed,
    pack,
    packs,
    kmat,
    amat,
    cmat,
    dmat,
    left,
    strip,
    own_b,
    all_b,
    part,
    parts_near,
    total,
    parts_far,
    load_sem,
    send_sem,
    recv_sem,
    m_send,
    m_recv,
    strip_send,
    strip_recv,
    share_send,
    share_recv,
    pack_send,
    pack_recv,
    b_send,
    b_recv,
    sum_send,
    sum_recv,
):
    ngx, ngy, ngrp = sizes
    groups = ngx * ngy
    devices = groups * ngrp
    wide = SPAN * ngrp * 16
    full = kmat.shape[0]
    rem, div = lax.rem, lax.div
    gx, gy, grp = (lax.axis_index(name) for name in ("gx", "gy", "grp"))
    group = gx * ngy + gy
    me = group * ngrp + grp

    def place(index):
        return (div(index, ngy * ngrp), rem(div(index, ngrp), ngy), rem(index, ngrp))

    before = place(rem(me + devices - 1, devices))
    after = place(rem(me + 1, devices))

    def gather_partner(i):
        turn = div(i, ngrp)
        half = div(turn + 1, 2)
        offset = half * (1 - 2 * rem(turn, 2))
        to_group = rem(group + offset + groups, groups)
        slot = (REACH - offset) * ngrp + grp
        return (div(to_group, ngy), rem(to_group, ngy), rem(grp + i, ngrp)), slot

    near_count = ngx * ngrp
    near_rank = gx * ngrp + grp

    def near_partner(i):
        rank = rem(near_rank + rem(near_count // 2 - 2 + i, near_count - 1) + 1, near_count)
        return (div(rank, ngrp), gy, rem(rank, ngrp))

    def far_partner(i):
        half = div(i, 2)
        return (gx, rem(gy + ngy // 2 + half * (2 * rem(i, 2) - 1) + ngy, ngy), grp)

    barrier = pltpu.get_barrier_semaphore()

    def greet(partner, count):
        def body(i, carry):
            pl.semaphore_signal(barrier, inc=1, device_id=partner(i), device_id_type=MESH)
            return carry

        lax.fori_loop(1, count, body, 0)

    greet(lambda i: gather_partner(i)[0], SPAN * ngrp)

    loads = []
    for i, (source, target) in enumerate(
        ((rhs_hbm, rhs), (inverses_hbm, inverses), (blocks_hbm, blocks), (basis_hbm, basis))
    ):
        copy = pltpu.make_async_copy(source, target, load_sem.at[i])
        copy.start()
        loads.append(copy)
    greet(near_partner, near_count)
    greet(far_partner, ngy)
    greetings = (SPAN * ngrp - 1) + (near_count - 1) + (ngy - 1)

    for side in range(2):
        chosen = [jnp.int32(0) for _ in range(HALO)]
        count = jnp.int32(0)
        for e in range(ELEMS):
            t = table[e, side]
            flag = (t >= 0) & (t < ELEMS) if side == 0 else t >= 2 * ELEMS
            chosen = [jnp.where(flag & (count == j), e, chosen[j]) for j in range(HALO)]
            count += flag.astype(jnp.int32)
        for j in range(HALO):
            give[side, j] = chosen[j]

    loads[0].wait()
    loads[1].wait()
    for e in range(ELEMS):
        pieces = jnp.concatenate(three(inverses[e]), axis=0)
        o = dot(pieces, rhs[e])
        q = o[0:64] + (o[64:128] + o[128:192])
        update[e] = q
        d = q * TAKE[0]
        direction[e] = d
        answer[e] = d

    pl.semaphore_wait(barrier, greetings)

    def ring(source, target, send, recv, side):
        return pltpu.make_async_remote_copy(
            src_ref=source,
            dst_ref=target,
            send_sem=send,
            recv_sem=recv,
            device_id=before if side == 0 else after,
            device_id_type=MESH,
        )

    pending = []

    def both(k, source, target, send, recv):
        copies = [ring(source.at[k, s], target.at[k, 1 - s], send.at[k, s], recv.at[k, s], s) for s in range(2)]
        for copy in copies:
            copy.start()
        pending.extend(copies)
        return copies

    def arrive(copies):
        for copy in copies:
            copy.wait_recv()

    def exchange(k, source):
        for side in range(2):
            for j in range(HALO):
                sent[k, side, j] = source[give[side, j]]
        return both(k, sent, landed, send_sem, recv_sem)

    def exchange_m(k, source):
        for side in range(2):
            for j in range(HALO):
                m_sent[k, side, j] = pltpu.roll(source[give[side, j]], 16 if side == 0 else LOADS - 16, 1)
        return both(k, m_sent, m_landed, m_send, m_recv)

    def store_pieces(ref, slot, value):
        high, middle, low = three(value)
        ref[slot, :, 0:128] = high
        ref[slot, :, 128:256] = middle
        ref[slot, :, 256:384] = low

    def cut(source, into):
        for e in range(ELEMS):
            store_pieces(into, e, source[e])

    def cut_halo(source, k, into):
        for side in range(2):
            for j in range(HALO):
                store_pieces(into, side * HALO + j, source[k, side, j])

    def products(matrix, stack):
        o = dot(matrix, stack[:, 0:256])
        p = dot(matrix[0:64], stack[:, 256:384])
        small = o[64:128, 128:256] + o[128:192, 0:128] + p
        return o[0:64, 0:128] + ((o[0:64, 128:256] + o[64:128, 0:128]) + small)

    def local_part(matrix, e, of):
        stack = jnp.concatenate([of[e]] + [of[near[e, k]] for k in range(6)], axis=0)
        return products(matrix[e], stack)

    def halo_part(matrix, e, of):
        stack = jnp.concatenate([of[far[e, 0]], of[far[e, 1]]], axis=0)
        return products(matrix[e, :, 64:192], stack)

    def gather(source, target, send, recv):
        own_slot = REACH * ngrp + grp

        def body(i, carry):
            device, slot = gather_partner(SPAN * ngrp - i)
            pltpu.make_async_remote_copy(
                src_ref=source,
                dst_ref=target.at[slot],
                send_sem=send,
                recv_sem=recv,
                device_id=device,
                device_id_type=MESH,
            ).start()
            return carry

        lax.fori_loop(1, SPAN * ngrp, body, 0)
        target[own_slot] = source[...]

    def wait_bytes(target, count, sem):
        pltpu.make_async_copy(target.at[pl.ds(0, count)], target.at[pl.ds(0, count)], sem).wait()

    gathered = SPAN * ngrp - 1

    copies = exchange(0, direction)

    loads[3].wait()
    first_lane = 16 * SIDE
    for e in range(ELEMS):
        spot = iota((16, MODES), 0) == iota((16, MODES), 1) + MODES * member[e]
        rows = exact(spot.astype(F32), basis[e])
        prolong_t[e] = rows
        tall = jnp.concatenate(
            [jnp.zeros((first_lane, NODES), F32), rows, jnp.zeros((112 - first_lane, NODES), F32)], axis=0
        )
        prolong[e] = tall.T
    copies_m = [exchange_m(0, prolong)]

    lanes = iota((8, 128), 1)
    for agg in range(2):
        row = iota((56, 128), 0)
        want = jnp.full((56, 128), 2 + agg, jnp.int32)
        for k in range(6):
            want = jnp.where(row // 8 == k + 1, coarse_table[agg, k], want)
        spot = iota((56, 128), 1) == want * 8 + row % 8
        t_rows = exact(coarse_blocks[agg], spot.astype(F32))
        small = iota((8, 128), 1) == iota((8, 128), 0) + 48 + 8 * agg
        d_rows = exact(coarse_inverses[agg], small.astype(F32))
        whole = coarse_map[agg]
        coarse_rows = group_inverse[whole]
        mine = owner[0, whole]
        kept = jnp.zeros((8, 64), F32)
        for c in range(8):
            same = (owner[0, c] == mine).astype(F32)
            kept = jnp.where(iota((8, 64), 1) // 8 == c, same, kept)
        shift = iota((64, 128), 1) == iota((64, 128), 0) + 64
        m_rows = exact(jnp.where(kept > 0.5, coarse_rows, 0.0), shift.astype(F32))
        s_rows = (lanes == iota((8, 128), 0) + 8 * whole).astype(F32)
        dt_rows = pltpu.roll(exact(coarse_inverses[agg], t_rows), 64, 1)
        first = jnp.where(lanes < 48, t_rows, jnp.where(lanes < 64, d_rows, m_rows))
        pack[8 * agg : 8 * agg + 8, 0:128] = first
        pack[8 * agg : 8 * agg + 8, 128:256] = jnp.where(lanes < 64, s_rows, dt_rows)
    gather(pack, packs, pack_send, pack_recv)

    for e in range(ELEMS):
        for k in range(6):
            t = table[e, k]
            here = (t >= ELEMS) & (t < 2 * ELEMS)
            near[e, k] = jnp.where(here, t - ELEMS, ELEMS)
    for side in range(2):
        chosen = [jnp.int32(0) for _ in range(HALO)]
        count = jnp.int32(0)
        for e in range(ELEMS):
            t = table[e, side]
            rank = jnp.int32(0)
            for other in range(ELEMS):
                u = table[other, side]
                lower = (u >= 0) & (u < t) if side == 0 else (u >= 2 * ELEMS) & (u < t)
                rank += lower.astype(jnp.int32)
            named = (t >= 0) & (t < ELEMS) if side == 0 else t >= 2 * ELEMS
            rank = jnp.minimum(rank, HALO - 1)
            far[e, side] = jnp.where(named, side * HALO + rank, 2 * HALO)
            chosen = [jnp.where(named & (rank == j), e, chosen[j]) for j in range(HALO)]
            count += named.astype(jnp.int32)
        for j in range(HALO):
            edge[side, j] = chosen[j]
        edge[side, HALO] = count
    window[ELEMS] = jnp.zeros((NODES, 3 * LOADS), BF16)
    window_m[ELEMS] = jnp.zeros((NODES, 3 * LOADS), BF16)
    halo[2 * HALO] = jnp.zeros((NODES, 3 * LOADS), BF16)
    halo_m[2 * HALO] = jnp.zeros((NODES, 3 * LOADS), BF16)

    loads[2].wait()
    for e in range(ELEMS):
        high, middle, low = three(exact(inverses[e], blocks[e]))
        da[e, 0:64] = high
        da[e, 64:128] = middle
        da[e, 128:192] = low

    def finish_step(k, copies, matrix, finish):
        arrive(copies)
        cut_halo(landed, k, halo)
        for e in range(ELEMS):
            finish(e, acc[e] + halo_part(matrix, e, halo))

    def local_step(matrix, source):
        cut(source, window)
        for e in range(ELEMS):
            acc[e] = local_part(matrix, e, window)

    def next_m(k, source, target):
        arrive(copies_m[k])
        cut(source, window_m)
        cut_halo(m_landed, k, halo_m)
        for e in range(ELEMS):
            target[e] = local_part(da, e, window_m) + halo_part(da, e, halo_m)

    def pre_finish(i):
        def finish(e, value):
            q = update[e] - value
            update[e] = q
            if i < 3:
                d = KEEP[i] * direction[e] + TAKE[i] * q
                direction[e] = d
                answer[e] = answer[e] + d
            else:
                field[e] = answer[e] + OMEGA * q

        return finish

    local_step(da, direction)
    for e in range(ELEMS):
        high, middle, low = three(blocks[e])
        a[e, 0:64] = high
        a[e, 64:128] = middle
        a[e, 128:192] = low
    for side in range(2):
        column = slice(64 + 64 * side, 128 + 64 * side)
        pieces = []
        for j in range(HALO):
            e = edge[side, j]
            rows = exact(prolong_t[e], blocks[e, :, column])
            pieces.append(jnp.where(edge[side, HALO] > j, rows, 0.0))
        strip_sent[0, side] = jnp.concatenate(pieces, axis=1)
    strip_copies = both(0, strip_sent, strip_landed, strip_send, strip_recv)
    finish_step(0, copies, da, pre_finish(1))

    copies = exchange(1, direction)
    next_m(0, prolong, m_one)
    copies_m.append(exchange_m(1, m_one))
    local_step(da, direction)

    wait_bytes(packs, gathered, pack_recv)
    wait_bytes(packs, gathered, pack_send)
    for ref in (kmat, amat, cmat, dmat):
        ref[...] = jnp.zeros((full, full), F32)
    blank = jnp.zeros((16, full - 128), F32)

    def spread(rows, first, count, move):
        keep = (iota((16, 128), 1) >= first) & (iota((16, 128), 1) < first + count)
        rows = jnp.concatenate([jnp.where(keep, rows, 0.0), blank], axis=1)
        return pltpu.roll(rows, (move - first) % full, 1)

    for w in range(SPAN * ngrp):
        one = packs[w, :, 0:128]
        two = packs[w, :, 128:256]
        here = slice(16 * w, 16 * w + 16)
        amat[here, :] = spread(one, 0, 48, 16 * (w - 1))
        dmat[here, :] = spread(one, 48, 16, 16 * w)
        kmat[here, :] = spread(two, 64, 48, 16 * (w - 1))
    for s in range(SPAN):
        parts = [packs[s * ngrp + j] for j in range(ngrp)]
        stacked = jnp.concatenate(parts, axis=0)
        coarse = stacked[:, 64:128]
        places = stacked[:, 128:192]
        block = lax.dot_general(
            coarse, places, (((1,), (1,)), ((), ())), preferred_element_type=F32, precision=HIGHEST
        )
        size = 16 * ngrp
        row = jnp.concatenate([block, jnp.zeros((size, full - size), F32)], axis=1)
        cmat[size * s : size * s + size, :] = pltpu.roll(row, size * s, 1) if s else row
    finish_step(1, copies, da, pre_finish(2))

    copies = exchange(2, direction)
    next_m(1, m_one, m_two)
    copies_m.append(exchange_m(2, m_two))
    local_step(da, direction)

    def smooth(rows):
        q = rows
        d = rows * TAKE[0]
        y = d
        for i in (1, 2):
            q = q - exact(d, kmat[...])
            d = KEEP[i] * d + TAKE[i] * q
            y = y + d
        return y

    held = 16 * (2 * SIDE + 1)
    start = (REACH * ngrp + grp - SIDE) * 16
    unit = (iota((128, full), 1) == iota((128, full), 0) + start) & (iota((128, full), 0) < held)
    unit = unit.astype(F32)
    u = smooth(unit)
    v = exact(u, kmat[...])
    strip[...] = v
    left[...] = 2.0 * u
    finish_step(2, copies, da, pre_finish(3))

    arrive(strip_copies)
    for side in range(2):
        edge_rows = jnp.concatenate([field[give[side, j]] for j in range(HALO)], axis=0)
        share_sent[0, side] = exact(strip_landed[0, side], edge_rows)
    share_copies = both(0, share_sent, share_landed, share_send, share_recv)
    copies = exchange(3, update)
    cut(field, window)
    mine_b = jnp.zeros((16, LOADS), F32)
    for e in range(ELEMS):
        acc[e] = rhs[e].astype(F32) - local_part(a, e, window)
    for e in range(ELEMS):
        mine_b = mine_b + exact(prolong_t[e], acc[e])
    next_m(2, m_two, m_three)
    local_step(da, update)
    arrive(share_copies)
    own_b[...] = mine_b - (share_landed[0, 0] + share_landed[0, 1])
    gather(own_b, all_b, b_send, b_recv)

    unit = (iota((128, full), 1) == iota((128, full), 0) + start) & (iota((128, full), 0) < held)
    m = exact(unit.astype(F32) - strip[...], cmat[...])
    y = smooth(strip[...] + exact(m, amat[...]))
    strip[...] = m + exact(left[...] - y, dmat[...])

    def post_first(e, value):
        q0 = update[e]
        d0 = TAKE[0] * q0
        q1 = q0 - TAKE[0] * value
        d1 = KEEP[1] * d0 + TAKE[1] * q1
        update[e] = q1
        direction[e] = d1
        answer[e] = answer[e] + d0 + d1

    finish_step(3, copies, da, post_first)

    for e in range(ELEMS):
        one, two = m_one[e], m_two[e]
        g = one - OMEGA * two
        h = g - TAKE[0] * (two - OMEGA * m_three[e])
        step = KEEP[1] * TAKE[0] * g + TAKE[1] * h
        whole = (prolong[e] - OMEGA * one) - TAKE[0] * g - step
        m_one[e] = step
        m_two[e] = h
        m_three[e] = whole

    wait_bytes(all_b, gathered, b_recv)
    values = all_b[...].reshape(wide, LOADS)
    padded = jnp.concatenate([values, jnp.zeros((full - wide, LOADS), F32)], axis=0)
    c = exact(strip[...], padded)
    rows = ELEMS * NODES
    change = exact(m_one[...].reshape(rows, LOADS), c).reshape(ELEMS, NODES, LOADS)
    direction[...] = direction[...] - change

    copies = exchange(4, direction)
    change = exact(m_two[...].reshape(rows, LOADS), c).reshape(ELEMS, NODES, LOADS)
    update[...] = update[...] - change
    change = exact(m_three[...].reshape(rows, LOADS), c).reshape(ELEMS, NODES, LOADS)
    answer[...] = answer[...] + change
    local_step(da, direction)
    wait_bytes(all_b, gathered, b_send)

    def post_last(e, value):
        q = update[e] - value
        answer[e] = answer[e] + (KEEP[2] * direction[e] + TAKE[2] * q)

    finish_step(4, copies, da, post_last)

    copies = exchange(5, answer)
    local_step(a, answer)
    sums = [jnp.zeros((8, LOADS), F32), jnp.zeros((8, LOADS), F32)]
    for e in range(ELEMS):
        x = answer[e]
        x_out[e] = x
        sums[0] = sums[0] + jnp.sum((rhs[e].astype(F32) * x).reshape(8, 8, LOADS), axis=0)

    def last(e, value):
        applied_out[e] = value
        sums[1] = sums[1] + jnp.sum((answer[e] * value).reshape(8, 8, LOADS), axis=0)

    finish_step(5, copies, a, last)
    row = iota((8, LOADS), 0)
    numerator = jnp.sum(sums[0], axis=0, keepdims=True)
    denominator = jnp.sum(sums[1], axis=0, keepdims=True)
    part[...] = jnp.where(row == 0, numerator, jnp.where(row == 1, denominator, 0.0))

    def combine(source, target, partner, rank, count, which):
        def body(i, carry):
            pltpu.make_async_remote_copy(
                src_ref=source,
                dst_ref=target.at[rank],
                send_sem=sum_send.at[which],
                recv_sem=sum_recv.at[which],
                device_id=partner(i),
                device_id_type=MESH,
            ).start()
            return carry

        lax.fori_loop(1, count, body, 0)
        target[rank] = source[...]
        wait_bytes(target, count - 1, sum_recv.at[which])
        return jnp.sum(target[...], axis=0)

    total[...] = combine(part, parts_near, near_partner, near_rank, near_count, 0)
    whole = combine(total, parts_far, far_partner, gy, ngy, 1)
    step_out[...] = jnp.broadcast_to(whole[0:1] / whole[1:2], (8, LOADS))
    wait_bytes(parts_near, near_count - 1, sum_send.at[0])
    wait_bytes(parts_far, ngy - 1, sum_send.at[1])
    for copy in pending:
        copy.wait_send()


def on_device(
    sizes,
    rhs,
    element_blocks,
    element_table,
    element_block_inverses,
    basis,
    element_aggregate,
    aggregate_blocks,
    aggregate_table,
    aggregate_inverse,
    coarse_map,
    coarse_owner,
    coarse_inverse,
):
    ngx, ngy, ngrp = sizes
    held = SPAN * ngrp
    full = -(-held * 16 // 128) * 128
    smem = pl.BlockSpec(memory_space=pltpu.SMEM)
    vmem = pl.BlockSpec(memory_space=pltpu.VMEM)
    hbm = pl.BlockSpec(memory_space=pltpu.HBM)
    shape = (ELEMS, NODES, LOADS)
    exchanges = 6
    cut_shape = (ELEMS + 1, NODES, 3 * LOADS)
    scratch = [
        pltpu.VMEM(shape, BF16),
        pltpu.VMEM((ELEMS, NODES, NODES), F32),
        pltpu.VMEM((ELEMS, NODES, 7 * NODES), F32),
        pltpu.VMEM((ELEMS, MODES, NODES), F32),
        pltpu.SMEM((ELEMS, 6), jnp.int32),
        pltpu.SMEM((ELEMS, 2), jnp.int32),
        pltpu.SMEM((2, HALO), jnp.int32),
        pltpu.SMEM((2, HALO + 1), jnp.int32),
        pltpu.VMEM((ELEMS, 192, 448), BF16),
        pltpu.VMEM((ELEMS, 192, 448), BF16),
        *([pltpu.VMEM(cut_shape, BF16)] * 4),
        *([pltpu.VMEM(shape, F32)] * 5),
        *([pltpu.VMEM((exchanges, 2, HALO, NODES, LOADS), F32)] * 2),
        pltpu.VMEM(shape, F32),
        pltpu.VMEM((ELEMS, 16, NODES), F32),
        *([pltpu.VMEM(shape, F32)] * 3),
        *([pltpu.VMEM((3, 2, HALO, NODES, LOADS), F32)] * 2),
        *([pltpu.VMEM((1, 2, 16, HALO * NODES), F32)] * 2),
        *([pltpu.VMEM((1, 2, 16, LOADS), F32)] * 2),
        pltpu.VMEM((16, 256), F32),
        pltpu.VMEM((held, 16, 256), F32),
        *([pltpu.VMEM((full, full), F32)] * 4),
        *([pltpu.VMEM((128, full), F32)] * 2),
        pltpu.VMEM((16, LOADS), F32),
        pltpu.VMEM((held, 16, LOADS), F32),
        pltpu.VMEM((8, LOADS), F32),
        pltpu.VMEM((ngx * ngrp, 8, LOADS), F32),
        pltpu.VMEM((8, LOADS), F32),
        pltpu.VMEM((ngy, 8, LOADS), F32),
        pltpu.SemaphoreType.DMA((4,)),
        *([pltpu.SemaphoreType.DMA((exchanges, 2))] * 2),
        *([pltpu.SemaphoreType.DMA((3, 2))] * 2),
        *([pltpu.SemaphoreType.DMA((1, 2))] * 4),
        *([pltpu.SemaphoreType.DMA] * 4),
        *([pltpu.SemaphoreType.DMA((2,))] * 2),
    ]
    x, applied, step = pl.pallas_call(
        functools.partial(kernel, sizes),
        out_shape=(
            jax.ShapeDtypeStruct(shape, F32),
            jax.ShapeDtypeStruct(shape, F32),
            jax.ShapeDtypeStruct((8, LOADS), F32),
        ),
        in_specs=[smem] * 5 + [hbm] * 4 + [vmem] * 3,
        out_specs=(vmem, vmem, vmem),
        scratch_shapes=scratch,
        compiler_params=pltpu.CompilerParams(
            collective_id=0, has_side_effects=True, vmem_limit_bytes=48 * 1024 * 1024
        ),
    )(
        element_table,
        element_aggregate,
        aggregate_table,
        coarse_map,
        coarse_owner,
        rhs,
        element_block_inverses,
        element_blocks,
        jnp.swapaxes(basis, 1, 2),
        aggregate_blocks,
        aggregate_inverse,
        coarse_inverse.reshape(8, 8, 64),
    )
    step = step[0:1][None]
    return step * x, rhs.astype(F32) - step * applied


def solution(mesh):
    sizes = tuple(mesh.shape[name] for name in ("gx", "gy", "grp"))
    slabs = P(("gx", "gy", "grp"), None, None)
    pairs = P(("gx", "gy", "grp"), None)
    ids = P(("gx", "gy", "grp"))
    return jax.shard_map(
        functools.partial(on_device, sizes),
        mesh=mesh,
        in_specs=(
            slabs,
            slabs,
            pairs,
            slabs,
            slabs,
            ids,
            slabs,
            pairs,
            slabs,
            ids,
            P(("gx", "gy"), None),
            P(("gx", "gy"), None, None),
        ),
        out_specs=(slabs, slabs),
        check_vma=False,
    )
```

```python
import functools

import jax
import jax.numpy as jnp
from jax import lax
from jax.experimental import pallas as pl
from jax.experimental.pallas import tpu as pltpu
from jax.sharding import PartitionSpec as P

OMEGA = 0.7
LOW_BOUND = 0.25
UPPER_LIMIT = 1.9
THETA = (UPPER_LIMIT + LOW_BOUND) / 2.0
DELTA = (UPPER_LIMIT - LOW_BOUND) / 2.0
SIGMA = THETA / DELTA
RHO = [1.0 / SIGMA]
for _ in range(2):
    RHO.append(1.0 / (2.0 * SIGMA - RHO[-1]))
KEEP = [0.0, RHO[1] * RHO[0], RHO[2] * RHO[1]]
TAKE = [1.0 / THETA, 2.0 * RHO[1] / DELTA, 2.0 * RHO[2] / DELTA]

ELEMS = 8
NODES = 64
MODES = 8
SIDE = 3
LOADS = 128
HALO = 4
REACH = 3
SPAN = 2 * REACH + 1
MESH = pl.DeviceIdType.MESH
HIGHEST = lax.Precision.HIGHEST
F32 = jnp.float32
BF16 = jnp.bfloat16


def dot(a, b):
    return jnp.dot(a, b, preferred_element_type=F32)


def exact(a, b):
    return jnp.dot(a, b, preferred_element_type=F32, precision=HIGHEST)


def three(v):
    high = v.astype(BF16)
    rest = v - high.astype(F32)
    middle = rest.astype(BF16)
    low = (rest - middle.astype(F32)).astype(BF16)
    return high, middle, low


def iota(shape, dim):
    return lax.broadcasted_iota(jnp.int32, shape, dim)


def kernel(
    sizes,
    table,
    member,
    coarse_table,
    coarse_map,
    owner,
    rhs_hbm,
    inverses_hbm,
    blocks_hbm,
    basis_hbm,
    coarse_blocks,
    coarse_inverses,
    group_inverse,
    x_out,
    applied_out,
    step_out,
    rhs,
    inverses,
    blocks,
    basis,
    near,
    far,
    give,
    edge,
    da,
    a,
    window,
    halo,
    window_m,
    halo_m,
    update,
    direction,
    answer,
    acc,
    field,
    sent,
    landed,
    prolong,
    prolong_t,
    m_one,
    m_two,
    m_three,
    m_sent,
    m_landed,
    strip_sent,
    strip_landed,
    share_sent,
    share_landed,
    pack,
    packs,
    kmat,
    amat,
    cmat,
    dmat,
    left,
    strip,
    own_b,
    all_b,
    part,
    parts_near,
    total,
    parts_far,
    load_sem,
    send_sem,
    recv_sem,
    m_send,
    m_recv,
    strip_send,
    strip_recv,
    share_send,
    share_recv,
    pack_send,
    pack_recv,
    b_send,
    b_recv,
    sum_send,
    sum_recv,
):
    ngx, ngy, ngrp = sizes
    groups = ngx * ngy
    devices = groups * ngrp
    wide = SPAN * ngrp * 16
    full = kmat.shape[0]
    rem, div = lax.rem, lax.div
    gx, gy, grp = (lax.axis_index(name) for name in ("gx", "gy", "grp"))
    group = gx * ngy + gy
    me = group * ngrp + grp

    def place(index):
        return (div(index, ngy * ngrp), rem(div(index, ngrp), ngy), rem(index, ngrp))

    before = place(rem(me + devices - 1, devices))
    after = place(rem(me + 1, devices))

    def gather_partner(i):
        turn = div(i, ngrp)
        half = div(turn + 1, 2)
        offset = half * (1 - 2 * rem(turn, 2))
        to_group = rem(group + offset + groups, groups)
        slot = (REACH - offset) * ngrp + grp
        return (div(to_group, ngy), rem(to_group, ngy), rem(grp + i, ngrp)), slot

    near_count = ngx * ngrp
    near_rank = gx * ngrp + grp

    def near_partner(i):
        rank = rem(near_rank + rem(near_count // 2 - 2 + i, near_count - 1) + 1, near_count)
        return (div(rank, ngrp), gy, rem(rank, ngrp))

    def far_partner(i):
        half = div(i, 2)
        return (gx, rem(gy + ngy // 2 + half * (2 * rem(i, 2) - 1) + ngy, ngy), grp)

    barrier = pltpu.get_barrier_semaphore()

    def greet(partner, count):
        def body(i, carry):
            pl.semaphore_signal(barrier, inc=1, device_id=partner(i), device_id_type=MESH)
            return carry

        lax.fori_loop(1, count, body, 0)

    greet(lambda i: gather_partner(i)[0], SPAN * ngrp)

    loads = []
    for i, (source, target) in enumerate(
        ((rhs_hbm, rhs), (inverses_hbm, inverses), (blocks_hbm, blocks), (basis_hbm, basis))
    ):
        copy = pltpu.make_async_copy(source, target, load_sem.at[i])
        copy.start()
        loads.append(copy)
    greet(near_partner, near_count)
    greet(far_partner, ngy)
    greetings = (SPAN * ngrp - 1) + (near_count - 1) + (ngy - 1)

    for side in range(2):
        chosen = [jnp.int32(0) for _ in range(HALO)]
        count = jnp.int32(0)
        for e in range(ELEMS):
            t = table[e, side]
            flag = (t >= 0) & (t < ELEMS) if side == 0 else t >= 2 * ELEMS
            chosen = [jnp.where(flag & (count == j), e, chosen[j]) for j in range(HALO)]
            count += flag.astype(jnp.int32)
        for j in range(HALO):
            give[side, j] = chosen[j]

    loads[0].wait()
    loads[1].wait()
    for e in range(ELEMS):
        pieces = jnp.concatenate(three(inverses[e]), axis=0)
        o = dot(pieces, rhs[e])
        q = o[0:64] + (o[64:128] + o[128:192])
        update[e] = q
        d = q * TAKE[0]
        direction[e] = d
        answer[e] = d

    pl.semaphore_wait(barrier, greetings)

    def ring(source, target, send, recv, side):
        return pltpu.make_async_remote_copy(
            src_ref=source,
            dst_ref=target,
            send_sem=send,
            recv_sem=recv,
            device_id=before if side == 0 else after,
            device_id_type=MESH,
        )

    pending = []

    def both(k, source, target, send, recv):
        copies = [ring(source.at[k, s], target.at[k, 1 - s], send.at[k, s], recv.at[k, s], s) for s in range(2)]
        for copy in copies:
            copy.start()
        pending.extend(copies)
        return copies

    def arrive(copies):
        for copy in copies:
            copy.wait_recv()

    def exchange(k, source):
        for side in range(2):
            for j in range(HALO):
                sent[k, side, j] = source[give[side, j]]
        return both(k, sent, landed, send_sem, recv_sem)

    def exchange_m(k, source):
        low, count = 16 * (SIDE - k), 16 * (2 * k + 1)
        copies = []
        for side in range(2):
            tall = jnp.concatenate([source[give[side, j]] for j in range(HALO)], axis=0)
            m_sent[k, side, 0:count] = tall.T[low : low + count]
            rows = pl.ds(0, count)
            copy = ring(
                m_sent.at[k, side, rows], m_landed.at[k, 1 - side, rows], m_send.at[k, side], m_recv.at[k, side], side
            )
            copy.start()
            copies.append(copy)
        pending.extend(copies)
        return copies

    def cut_halo_m(k):
        low, count = 16 * (SIDE - k), 16 * (2 * k + 1)
        for side in range(2):
            first = low - 16 if side == 0 else low + 16
            rows = [m_landed[k, side, 0:count], jnp.zeros((LOADS - first - count, HALO * NODES), F32)]
            if first:
                rows = [jnp.zeros((first, HALO * NODES), F32)] + rows
            tall = jnp.concatenate(rows, axis=0).T
            for j in range(HALO):
                store_pieces(halo_m, side * HALO + j, tall[NODES * j : NODES * j + NODES])

    def store_pieces(ref, slot, value):
        high, middle, low = three(value)
        ref[slot, :, 0:128] = high
        ref[slot, :, 128:256] = middle
        ref[slot, :, 256:384] = low

    def cut(source, into):
        for e in range(ELEMS):
            store_pieces(into, e, source[e])

    def cut_halo(source, k, into):
        for side in range(2):
            for j in range(HALO):
                store_pieces(into, side * HALO + j, source[k, side, j])

    def products(matrix, stack):
        o = dot(matrix, stack[:, 0:256])
        p = dot(matrix[0:64], stack[:, 256:384])
        small = o[64:128, 128:256] + o[128:192, 0:128] + p
        return o[0:64, 0:128] + ((o[0:64, 128:256] + o[64:128, 0:128]) + small)

    def local_part(matrix, e, of):
        stack = jnp.concatenate([of[e]] + [of[near[e, k]] for k in range(6)], axis=0)
        return products(matrix[e], stack)

    def halo_part(matrix, e, of):
        stack = jnp.concatenate([of[far[e, 0]], of[far[e, 1]]], axis=0)
        return products(matrix[e, :, 64:192], stack)

    def gather(source, target, send, recv, first, stop):

        def body(i, carry):
            device, slot = gather_partner(SPAN * ngrp - i)
            pltpu.make_async_remote_copy(
                src_ref=source,
                dst_ref=target.at[slot],
                send_sem=send,
                recv_sem=recv,
                device_id=device,
                device_id_type=MESH,
            ).start()
            return carry

        lax.fori_loop(first, stop, body, 0)

    def wait_bytes(target, count, sem):
        pltpu.make_async_copy(target.at[pl.ds(0, count)], target.at[pl.ds(0, count)], sem).wait()

    gathered = SPAN * ngrp - 1

    copies = exchange(0, direction)

    loads[3].wait()
    first_lane = 16 * SIDE
    for e in range(ELEMS):
        spot = iota((16, MODES), 0) == iota((16, MODES), 1) + MODES * member[e]
        rows = exact(spot.astype(F32), basis[e])
        prolong_t[e] = rows
        tall = jnp.concatenate(
            [jnp.zeros((first_lane, NODES), F32), rows, jnp.zeros((112 - first_lane, NODES), F32)], axis=0
        )
        prolong[e] = tall.T
    copies_m = [exchange_m(0, prolong)]

    lanes = iota((8, 128), 1)
    for agg in range(2):
        row = iota((56, 128), 0)
        want = jnp.full((56, 128), 2 + agg, jnp.int32)
        for k in range(6):
            want = jnp.where(row // 8 == k + 1, coarse_table[agg, k], want)
        spot = iota((56, 128), 1) == want * 8 + row % 8
        t_rows = exact(coarse_blocks[agg], spot.astype(F32))
        small = iota((8, 128), 1) == iota((8, 128), 0) + 48
        d_rows = exact(coarse_inverses[agg], small.astype(F32))
        whole = coarse_map[agg]
        coarse_rows = group_inverse[whole]
        mine = owner[0, whole]
        kept = jnp.zeros((8, 64), F32)
        for c in range(8):
            same = (owner[0, c] == mine).astype(F32)
            kept = jnp.where(iota((8, 64), 1) // 8 == c, same, kept)
        shift = iota((64, 128), 1) == iota((64, 128), 0) + 64
        m_rows = exact(jnp.where(kept > 0.5, coarse_rows, 0.0), shift.astype(F32))
        place_rows = jnp.where(lanes == 56, whole.astype(F32), m_rows)
        first = jnp.where(lanes < 48, t_rows, jnp.where(lanes < 56, d_rows, place_rows))
        pack[8 * agg : 8 * agg + 8] = first
    half_way = SPAN * ngrp // 2
    packs[REACH * ngrp + grp] = pack[...]
    gather(pack, packs, pack_send, pack_recv, 1, half_way)

    for e in range(ELEMS):
        for k in range(6):
            t = table[e, k]
            here = (t >= ELEMS) & (t < 2 * ELEMS)
            near[e, k] = jnp.where(here, t - ELEMS, ELEMS)
    for side in range(2):
        chosen = [jnp.int32(0) for _ in range(HALO)]
        count = jnp.int32(0)
        for e in range(ELEMS):
            t = table[e, side]
            rank = jnp.int32(0)
            for other in range(ELEMS):
                u = table[other, side]
                lower = (u >= 0) & (u < t) if side == 0 else (u >= 2 * ELEMS) & (u < t)
                rank += lower.astype(jnp.int32)
            named = (t >= 0) & (t < ELEMS) if side == 0 else t >= 2 * ELEMS
            rank = jnp.minimum(rank, HALO - 1)
            far[e, side] = jnp.where(named, side * HALO + rank, 2 * HALO)
            chosen = [jnp.where(named & (rank == j), e, chosen[j]) for j in range(HALO)]
            count += named.astype(jnp.int32)
        for j in range(HALO):
            edge[side, j] = chosen[j]
        edge[side, HALO] = count
    window[ELEMS] = jnp.zeros((NODES, 3 * LOADS), BF16)
    window_m[ELEMS] = jnp.zeros((NODES, 3 * LOADS), BF16)
    halo[2 * HALO] = jnp.zeros((NODES, 3 * LOADS), BF16)
    halo_m[2 * HALO] = jnp.zeros((NODES, 3 * LOADS), BF16)

    loads[2].wait()
    for e in range(ELEMS):
        high, middle, low = three(exact(inverses[e], blocks[e]))
        da[e, 0:64] = high
        da[e, 64:128] = middle
        da[e, 128:192] = low

    def finish_step(k, copies, matrix, finish):
        arrive(copies)
        cut_halo(landed, k, halo)
        for e in range(ELEMS):
            finish(e, acc[e] + halo_part(matrix, e, halo))

    def local_step(matrix, source):
        cut(source, window)
        for e in range(ELEMS):
            acc[e] = local_part(matrix, e, window)

    def next_m(k, source, target):
        arrive(copies_m[k])
        cut(source, window_m)
        cut_halo_m(k)
        for e in range(ELEMS):
            target[e] = local_part(da, e, window_m) + halo_part(da, e, halo_m)

    def pre_finish(i):
        def finish(e, value):
            q = update[e] - value
            update[e] = q
            if i < 3:
                d = KEEP[i] * direction[e] + TAKE[i] * q
                direction[e] = d
                answer[e] = answer[e] + d
            else:
                field[e] = answer[e] + OMEGA * q

        return finish

    local_step(da, direction)
    for e in range(ELEMS):
        high, middle, low = three(blocks[e])
        a[e, 0:64] = high
        a[e, 64:128] = middle
        a[e, 128:192] = low
    for side in range(2):
        column = slice(64 + 64 * side, 128 + 64 * side)
        pieces = []
        for j in range(HALO):
            e = edge[side, j]
            rows = exact(prolong_t[e], blocks[e, :, column])
            pieces.append(jnp.where(edge[side, HALO] > j, rows, 0.0))
        strip_sent[0, side] = jnp.concatenate(pieces, axis=1)
    strip_copies = both(0, strip_sent, strip_landed, strip_send, strip_recv)
    finish_step(0, copies, da, pre_finish(1))

    copies = exchange(1, direction)
    next_m(0, prolong, m_one)
    copies_m.append(exchange_m(1, m_one))
    gather(pack, packs, pack_send, pack_recv, half_way, SPAN * ngrp)
    local_step(da, direction)

    finish_step(1, copies, da, pre_finish(2))

    copies = exchange(2, direction)
    next_m(1, m_one, m_two)
    copies_m.append(exchange_m(2, m_two))
    local_step(da, direction)

    wait_bytes(packs, gathered, pack_recv)
    wait_bytes(packs, gathered, pack_send)
    for ref in (kmat, amat, cmat, dmat):
        ref[...] = jnp.zeros((full, full), F32)

    def spread(rows, first, count, move):
        lane = iota(rows.shape, 1)
        rows = jnp.where((lane >= first) & (lane < first + count), rows, 0.0)
        rows = jnp.concatenate([rows, jnp.zeros((rows.shape[0], full - 128), F32)], axis=1)
        return pltpu.roll(rows, (move - first) % full, 1)

    for w in range(SPAN * ngrp):
        one = packs[w]
        amat[16 * w : 16 * w + 16, :] = spread(one, 0, 48, 16 * (w - 1))
        for agg in range(2):
            at = 16 * w + 8 * agg
            dmat[at : at + 8, :] = spread(one[8 * agg : 8 * agg + 8], 48, 8, at)
    tall = packs[...].reshape(wide, 128)
    tall = jnp.where(iota((wide, 128), 1) < 48, tall, 0.0)
    tall = exact(dmat[...], jnp.concatenate([tall, jnp.zeros((full - wide, 128), F32)], axis=0))
    for w in range(SPAN * ngrp):
        kmat[16 * w : 16 * w + 16, :] = spread(tall[16 * w : 16 * w + 16], 0, 48, 16 * (w - 1))
    size = 16 * ngrp
    for s in range(SPAN):
        stacked = jnp.concatenate([packs[s * ngrp + j] for j in range(ngrp)], axis=0)
        coarse = stacked[:, 64:128]
        target = 8.0 * stacked[:, 56:57] + (iota((size, 64), 0) % 8).astype(F32)
        places = jnp.where(jnp.abs(iota((size, 64), 1).astype(F32) - target) < 0.5, 1.0, 0.0)
        block = lax.dot_general(
            coarse, places, (((1,), (1,)), ((), ())), preferred_element_type=F32, precision=HIGHEST
        )
        row = jnp.concatenate([block, jnp.zeros((size, full - size), F32)], axis=1)
        cmat[size * s : size * s + size, :] = pltpu.roll(row, size * s, 1) if s else row
    finish_step(2, copies, da, pre_finish(3))

    arrive(strip_copies)
    for side in range(2):
        edge_rows = jnp.concatenate([field[give[side, j]] for j in range(HALO)], axis=0)
        share_sent[0, side] = exact(strip_landed[0, side], edge_rows)
    share_copies = both(0, share_sent, share_landed, share_send, share_recv)
    copies = exchange(3, update)
    cut(field, window)
    mine_b = jnp.zeros((16, LOADS), F32)
    for e in range(ELEMS):
        acc[e] = rhs[e].astype(F32) - local_part(a, e, window)
    for e in range(ELEMS):
        mine_b = mine_b + exact(prolong_t[e], acc[e])
    def smooth(rows):
        q = rows
        d = rows * TAKE[0]
        y = d
        for i in (1, 2):
            q = q - exact(d, kmat[...])
            d = KEEP[i] * d + TAKE[i] * q
            y = y + d
        return y

    held = 16 * (2 * SIDE + 1)
    start = (REACH * ngrp + grp - SIDE) * 16
    unit = (iota((128, full), 1) == iota((128, full), 0) + start) & (iota((128, full), 0) < held)
    unit = unit.astype(F32)
    u = smooth(unit)
    v = exact(u, kmat[...])
    strip[...] = v
    left[...] = 2.0 * u

    next_m(2, m_two, m_three)
    arrive(share_copies)
    own_b[...] = mine_b - (share_landed[0, 0] + share_landed[0, 1])
    gather(own_b, all_b, b_send, b_recv, 1, SPAN * ngrp)
    all_b[REACH * ngrp + grp] = own_b[...]

    local_step(da, update)
    unit = (iota((128, full), 1) == iota((128, full), 0) + start) & (iota((128, full), 0) < held)
    m = exact(unit.astype(F32) - strip[...], cmat[...])
    y = smooth(strip[...] + exact(m, amat[...]))
    strip[...] = m + exact(left[...] - y, dmat[...])

    def post_first(e, value):
        q0 = update[e]
        d0 = TAKE[0] * q0
        q1 = q0 - TAKE[0] * value
        d1 = KEEP[1] * d0 + TAKE[1] * q1
        update[e] = q1
        direction[e] = d1
        answer[e] = answer[e] + d0 + d1

    finish_step(3, copies, da, post_first)

    for e in range(ELEMS):
        one, two = m_one[e], m_two[e]
        g = one - OMEGA * two
        h = g - TAKE[0] * (two - OMEGA * m_three[e])
        step = KEEP[1] * TAKE[0] * g + TAKE[1] * h
        whole = (prolong[e] - OMEGA * one) - TAKE[0] * g - step
        m_one[e] = step
        m_two[e] = h
        m_three[e] = whole

    wait_bytes(all_b, gathered, b_recv)
    values = all_b[...].reshape(wide, LOADS)
    padded = jnp.concatenate([values, jnp.zeros((full - wide, LOADS), F32)], axis=0)
    c = exact(strip[...], padded)
    rows = ELEMS * NODES
    change = exact(m_one[...].reshape(rows, LOADS), c).reshape(ELEMS, NODES, LOADS)
    direction[...] = direction[...] - change

    copies = exchange(4, direction)
    change = exact(m_two[...].reshape(rows, LOADS), c).reshape(ELEMS, NODES, LOADS)
    update[...] = update[...] - change
    change = exact(m_three[...].reshape(rows, LOADS), c).reshape(ELEMS, NODES, LOADS)
    answer[...] = answer[...] + change
    local_step(da, direction)
    wait_bytes(all_b, gathered, b_send)

    def post_last(e, value):
        q = update[e] - value
        answer[e] = answer[e] + (KEEP[2] * direction[e] + TAKE[2] * q)

    finish_step(4, copies, da, post_last)

    copies = exchange(5, answer)
    local_step(a, answer)
    sums = [jnp.zeros((8, LOADS), F32), jnp.zeros((8, LOADS), F32)]
    for e in range(ELEMS):
        x = answer[e]
        x_out[e] = x
        sums[0] = sums[0] + jnp.sum((rhs[e].astype(F32) * x).reshape(8, 8, LOADS), axis=0)

    def last(e, value):
        applied_out[e] = value
        sums[1] = sums[1] + jnp.sum((answer[e] * value).reshape(8, 8, LOADS), axis=0)

    finish_step(5, copies, a, last)
    row = iota((8, LOADS), 0)
    numerator = jnp.sum(sums[0], axis=0, keepdims=True)
    denominator = jnp.sum(sums[1], axis=0, keepdims=True)
    part[...] = jnp.where(row == 0, numerator, jnp.where(row == 1, denominator, 0.0))

    def combine(source, target, partner, rank, count, which):
        def body(i, carry):
            pltpu.make_async_remote_copy(
                src_ref=source,
                dst_ref=target.at[rank],
                send_sem=sum_send.at[which],
                recv_sem=sum_recv.at[which],
                device_id=partner(i),
                device_id_type=MESH,
            ).start()
            return carry

        lax.fori_loop(1, count, body, 0)
        target[rank] = source[...]
        wait_bytes(target, count - 1, sum_recv.at[which])
        return jnp.sum(target[...], axis=0)

    total[...] = combine(part, parts_near, near_partner, near_rank, near_count, 0)
    whole = combine(total, parts_far, far_partner, gy, ngy, 1)
    step_out[...] = jnp.broadcast_to(whole[0:1] / whole[1:2], (8, LOADS))
    wait_bytes(parts_near, near_count - 1, sum_send.at[0])
    wait_bytes(parts_far, ngy - 1, sum_send.at[1])
    for copy in pending:
        copy.wait_send()


def on_device(
    sizes,
    rhs,
    element_blocks,
    element_table,
    element_block_inverses,
    basis,
    element_aggregate,
    aggregate_blocks,
    aggregate_table,
    aggregate_inverse,
    coarse_map,
    coarse_owner,
    coarse_inverse,
):
    ngx, ngy, ngrp = sizes
    held = SPAN * ngrp
    full = -(-held * 16 // 128) * 128
    smem = pl.BlockSpec(memory_space=pltpu.SMEM)
    vmem = pl.BlockSpec(memory_space=pltpu.VMEM)
    hbm = pl.BlockSpec(memory_space=pltpu.HBM)
    shape = (ELEMS, NODES, LOADS)
    exchanges = 6
    cut_shape = (ELEMS + 1, NODES, 3 * LOADS)
    scratch = [
        pltpu.VMEM(shape, BF16),
        pltpu.VMEM((ELEMS, NODES, NODES), F32),
        pltpu.VMEM((ELEMS, NODES, 7 * NODES), F32),
        pltpu.VMEM((ELEMS, MODES, NODES), F32),
        pltpu.SMEM((ELEMS, 6), jnp.int32),
        pltpu.SMEM((ELEMS, 2), jnp.int32),
        pltpu.SMEM((2, HALO), jnp.int32),
        pltpu.SMEM((2, HALO + 1), jnp.int32),
        pltpu.VMEM((ELEMS, 192, 448), BF16),
        pltpu.VMEM((ELEMS, 192, 448), BF16),
        *([pltpu.VMEM(cut_shape, BF16)] * 4),
        *([pltpu.VMEM(shape, F32)] * 5),
        *([pltpu.VMEM((exchanges, 2, HALO, NODES, LOADS), F32)] * 2),
        pltpu.VMEM(shape, F32),
        pltpu.VMEM((ELEMS, 16, NODES), F32),
        *([pltpu.VMEM(shape, F32)] * 3),
        *([pltpu.VMEM((3, 2, 16 * (2 * SIDE - 1), HALO * NODES), F32)] * 2),
        *([pltpu.VMEM((1, 2, 16, HALO * NODES), F32)] * 2),
        *([pltpu.VMEM((1, 2, 16, LOADS), F32)] * 2),
        pltpu.VMEM((16, LOADS), F32),
        pltpu.VMEM((held, 16, LOADS), F32),
        *([pltpu.VMEM((full, full), F32)] * 4),
        *([pltpu.VMEM((128, full), F32)] * 2),
        pltpu.VMEM((16, LOADS), F32),
        pltpu.VMEM((held, 16, LOADS), F32),
        pltpu.VMEM((8, LOADS), F32),
        pltpu.VMEM((ngx * ngrp, 8, LOADS), F32),
        pltpu.VMEM((8, LOADS), F32),
        pltpu.VMEM((ngy, 8, LOADS), F32),
        pltpu.SemaphoreType.DMA((4,)),
        *([pltpu.SemaphoreType.DMA((exchanges, 2))] * 2),
        *([pltpu.SemaphoreType.DMA((3, 2))] * 2),
        *([pltpu.SemaphoreType.DMA((1, 2))] * 4),
        *([pltpu.SemaphoreType.DMA] * 4),
        *([pltpu.SemaphoreType.DMA((2,))] * 2),
    ]
    x, applied, step = pl.pallas_call(
        functools.partial(kernel, sizes),
        out_shape=(
            jax.ShapeDtypeStruct(shape, F32),
            jax.ShapeDtypeStruct(shape, F32),
            jax.ShapeDtypeStruct((8, LOADS), F32),
        ),
        in_specs=[smem] * 5 + [hbm] * 4 + [vmem] * 3,
        out_specs=(vmem, vmem, vmem),
        scratch_shapes=scratch,
        compiler_params=pltpu.CompilerParams(
            collective_id=0, has_side_effects=True, vmem_limit_bytes=48 * 1024 * 1024
        ),
    )(
        element_table,
        element_aggregate,
        aggregate_table,
        coarse_map,
        coarse_owner,
        rhs,
        element_block_inverses,
        element_blocks,
        jnp.swapaxes(basis, 1, 2),
        aggregate_blocks,
        aggregate_inverse,
        coarse_inverse.reshape(8, 8, 64),
    )
    step = step[0:1][None]
    return step * x, rhs.astype(F32) - step * applied


def solution(mesh):
    sizes = tuple(mesh.shape[name] for name in ("gx", "gy", "grp"))
    slabs = P(("gx", "gy", "grp"), None, None)
    pairs = P(("gx", "gy", "grp"), None)
    ids = P(("gx", "gy", "grp"))
    return jax.shard_map(
        functools.partial(on_device, sizes),
        mesh=mesh,
        in_specs=(
            slabs,
            slabs,
            pairs,
            slabs,
            slabs,
            ids,
            slabs,
            pairs,
            slabs,
            ids,
            P(("gx", "gy"), None),
            P(("gx", "gy"), None, None),
        ),
        out_specs=(slabs, slabs),
        check_vma=False,
    )
```

```python
import functools

import jax
import jax.numpy as jnp
from jax import lax
from jax.experimental import pallas as pl
from jax.experimental.pallas import tpu as pltpu
from jax.sharding import PartitionSpec as P

OMEGA = 0.7
LOW_BOUND = 0.25
UPPER_LIMIT = 1.9
THETA = (UPPER_LIMIT + LOW_BOUND) / 2.0
DELTA = (UPPER_LIMIT - LOW_BOUND) / 2.0
SIGMA = THETA / DELTA
RHO = [1.0 / SIGMA]
for _ in range(2):
    RHO.append(1.0 / (2.0 * SIGMA - RHO[-1]))
KEEP = [0.0, RHO[1] * RHO[0], RHO[2] * RHO[1]]
TAKE = [1.0 / THETA, 2.0 * RHO[1] / DELTA, 2.0 * RHO[2] / DELTA]

ELEMS = 8
NODES = 64
MODES = 8
SIDE = 3
LOADS = 128
HALO = 4
REACH = 3
SPAN = 2 * REACH + 1
MESH = pl.DeviceIdType.MESH
HIGHEST = lax.Precision.HIGHEST
F32 = jnp.float32
BF16 = jnp.bfloat16


def dot(a, b):
    return jnp.dot(a, b, preferred_element_type=F32)


def exact(a, b):
    return jnp.dot(a, b, preferred_element_type=F32, precision=HIGHEST)


def three(v):
    high = v.astype(BF16)
    rest = v - high.astype(F32)
    middle = rest.astype(BF16)
    low = (rest - middle.astype(F32)).astype(BF16)
    return high, middle, low


def iota(shape, dim):
    return lax.broadcasted_iota(jnp.int32, shape, dim)


def kernel(
    sizes,
    table,
    member,
    coarse_table,
    coarse_map,
    owner,
    rhs_hbm,
    inverses_hbm,
    blocks_hbm,
    basis_hbm,
    coarse_blocks,
    coarse_inverses,
    group_inverse,
    x_out,
    applied_out,
    step_out,
    rhs,
    inverses,
    blocks,
    basis,
    near,
    far,
    give,
    edge,
    da,
    a,
    window,
    halo,
    window_m,
    halo_m,
    update,
    direction,
    answer,
    acc,
    field,
    sent,
    landed,
    prolong,
    prolong_t,
    m_one,
    m_two,
    m_three,
    m_sent,
    m_landed,
    strip_sent,
    strip_landed,
    share_sent,
    share_landed,
    pack,
    packs,
    kmat,
    amat,
    cmat,
    dmat,
    left,
    strip,
    own_b,
    all_b,
    part,
    parts_near,
    total,
    parts_far,
    load_sem,
    send_sem,
    recv_sem,
    m_send,
    m_recv,
    strip_send,
    strip_recv,
    share_send,
    share_recv,
    pack_send,
    pack_recv,
    b_send,
    b_recv,
    sum_send,
    sum_recv,
):
    ngx, ngy, ngrp = sizes
    groups = ngx * ngy
    devices = groups * ngrp
    wide = SPAN * ngrp * 16
    full = kmat.shape[0]
    rem, div = lax.rem, lax.div
    gx, gy, grp = (lax.axis_index(name) for name in ("gx", "gy", "grp"))
    group = gx * ngy + gy
    me = group * ngrp + grp

    def place(index):
        return (div(index, ngy * ngrp), rem(div(index, ngrp), ngy), rem(index, ngrp))

    before = place(rem(me + devices - 1, devices))
    after = place(rem(me + 1, devices))

    def gather_partner(i):
        turn = div(i, ngrp)
        half = div(turn + 1, 2)
        offset = half * (1 - 2 * rem(turn, 2))
        to_group = rem(group + offset + groups, groups)
        slot = (REACH - offset) * ngrp + grp
        return (div(to_group, ngy), rem(to_group, ngy), rem(grp + i, ngrp)), slot

    near_count = ngx * ngrp
    near_rank = gx * ngrp + grp

    def near_partner(i):
        rank = rem(near_rank + rem(near_count // 2 - 2 + i, near_count - 1) + 1, near_count)
        return (div(rank, ngrp), gy, rem(rank, ngrp))

    def far_partner(i):
        half = div(i, 2)
        return (gx, rem(gy + ngy // 2 + half * (2 * rem(i, 2) - 1) + ngy, ngy), grp)

    barrier = pltpu.get_barrier_semaphore()

    def greet(partner, count):
        def body(i, carry):
            pl.semaphore_signal(barrier, inc=1, device_id=partner(i), device_id_type=MESH)
            return carry

        lax.fori_loop(1, count, body, 0, unroll=True)

    greet(lambda i: gather_partner(i)[0], SPAN * ngrp)

    loads = []
    for i, (source, target) in enumerate(
        ((rhs_hbm, rhs), (inverses_hbm, inverses), (blocks_hbm, blocks), (basis_hbm, basis))
    ):
        copy = pltpu.make_async_copy(source, target, load_sem.at[i])
        copy.start()
        loads.append(copy)
    greet(near_partner, near_count)
    greet(far_partner, ngy)
    greetings = (SPAN * ngrp - 1) + (near_count - 1) + (ngy - 1)

    for side in range(2):
        chosen = [jnp.int32(0) for _ in range(HALO)]
        count = jnp.int32(0)
        for e in range(ELEMS):
            t = table[e, side]
            flag = (t >= 0) & (t < ELEMS) if side == 0 else t >= 2 * ELEMS
            chosen = [jnp.where(flag & (count == j), e, chosen[j]) for j in range(HALO)]
            count += flag.astype(jnp.int32)
        for j in range(HALO):
            give[side, j] = chosen[j]

    loads[0].wait()
    loads[1].wait()
    for e in range(ELEMS):
        pieces = jnp.concatenate(three(inverses[e]), axis=0)
        o = dot(pieces, rhs[e])
        q = o[0:64] + (o[64:128] + o[128:192])
        update[e] = q
        d = q * TAKE[0]
        direction[e] = d
        answer[e] = d

    pl.semaphore_wait(barrier, greetings)

    def ring(source, target, send, recv, side):
        return pltpu.make_async_remote_copy(
            src_ref=source,
            dst_ref=target,
            send_sem=send,
            recv_sem=recv,
            device_id=before if side == 0 else after,
            device_id_type=MESH,
        )

    pending = []

    def both(k, source, target, send, recv):
        copies = [ring(source.at[k, s], target.at[k, 1 - s], send.at[k, s], recv.at[k, s], s) for s in range(2)]
        for copy in copies:
            copy.start()
        pending.extend(copies)
        return copies

    def arrive(copies):
        for copy in copies:
            copy.wait_recv()

    def exchange(k, source):
        for side in range(2):
            for j in range(HALO):
                sent[k, side, j] = source[give[side, j]]
        return both(k, sent, landed, send_sem, recv_sem)

    def exchange_m(k, source):
        low, count = 16 * (SIDE - k), 16 * (2 * k + 1)
        copies = []
        for side in range(2):
            tall = jnp.concatenate([source[give[side, j]] for j in range(HALO)], axis=0)
            m_sent[k, side, 0:count] = tall.T[low : low + count]
            rows = pl.ds(0, count)
            copy = ring(
                m_sent.at[k, side, rows], m_landed.at[k, 1 - side, rows], m_send.at[k, side], m_recv.at[k, side], side
            )
            copy.start()
            copies.append(copy)
        pending.extend(copies)
        return copies

    def cut_halo_m(k):
        low, count = 16 * (SIDE - k), 16 * (2 * k + 1)
        for side in range(2):
            first = low - 16 if side == 0 else low + 16
            rows = [m_landed[k, side, 0:count], jnp.zeros((LOADS - first - count, HALO * NODES), F32)]
            if first:
                rows = [jnp.zeros((first, HALO * NODES), F32)] + rows
            tall = jnp.concatenate(rows, axis=0).T
            for j in range(HALO):
                store_pieces(halo_m, side * HALO + j, tall[NODES * j : NODES * j + NODES])

    def store_pieces(ref, slot, value):
        high, middle, low = three(value)
        ref[slot, :, 0:128] = high
        ref[slot, :, 128:256] = middle
        ref[slot, :, 256:384] = low

    def cut(source, into):
        for e in range(ELEMS):
            store_pieces(into, e, source[e])

    def cut_halo(source, k, into):
        for side in range(2):
            for j in range(HALO):
                store_pieces(into, side * HALO + j, source[k, side, j])

    def products(matrix, stack):
        o = dot(matrix, stack[:, 0:256])
        p = dot(matrix[0:64], stack[:, 256:384])
        small = o[64:128, 128:256] + o[128:192, 0:128] + p
        return o[0:64, 0:128] + ((o[0:64, 128:256] + o[64:128, 0:128]) + small)

    def local_part(matrix, e, of):
        stack = jnp.concatenate([of[e]] + [of[near[e, k]] for k in range(6)], axis=0)
        return products(matrix[e], stack)

    def halo_part(matrix, e, of):
        stack = jnp.concatenate([of[far[e, 0]], of[far[e, 1]]], axis=0)
        return products(matrix[e, :, 64:192], stack)

    def gather(source, target, send, recv, first, stop):

        def body(i, carry):
            device, slot = gather_partner(SPAN * ngrp - i)
            pltpu.make_async_remote_copy(
                src_ref=source,
                dst_ref=target.at[slot],
                send_sem=send,
                recv_sem=recv,
                device_id=device,
                device_id_type=MESH,
            ).start()
            return carry

        lax.fori_loop(first, stop, body, 0)

    def wait_bytes(target, count, sem):
        pltpu.make_async_copy(target.at[pl.ds(0, count)], target.at[pl.ds(0, count)], sem).wait()

    gathered = SPAN * ngrp - 1

    copies = exchange(0, direction)

    loads[3].wait()
    first_lane = 16 * SIDE
    for e in range(ELEMS):
        spot = iota((16, MODES), 0) == iota((16, MODES), 1) + MODES * member[e]
        rows = exact(spot.astype(F32), basis[e])
        prolong_t[e] = rows
        tall = jnp.concatenate(
            [jnp.zeros((first_lane, NODES), F32), rows, jnp.zeros((112 - first_lane, NODES), F32)], axis=0
        )
        prolong[e] = tall.T
    copies_m = [exchange_m(0, prolong)]

    lanes = iota((8, 128), 1)
    for agg in range(2):
        row = iota((56, 128), 0)
        want = jnp.full((56, 128), 2 + agg, jnp.int32)
        for k in range(6):
            want = jnp.where(row // 8 == k + 1, coarse_table[agg, k], want)
        spot = iota((56, 128), 1) == want * 8 + row % 8
        t_rows = exact(coarse_blocks[agg], spot.astype(F32))
        small = iota((8, 128), 1) == iota((8, 128), 0) + 48
        d_rows = exact(coarse_inverses[agg], small.astype(F32))
        whole = coarse_map[agg]
        coarse_rows = group_inverse[whole]
        mine = owner[0, whole]
        kept = jnp.zeros((8, 64), F32)
        for c in range(8):
            same = (owner[0, c] == mine).astype(F32)
            kept = jnp.where(iota((8, 64), 1) // 8 == c, same, kept)
        shift = iota((64, 128), 1) == iota((64, 128), 0) + 64
        m_rows = exact(jnp.where(kept > 0.5, coarse_rows, 0.0), shift.astype(F32))
        place_rows = jnp.where(lanes == 56, whole.astype(F32), m_rows)
        first = jnp.where(lanes < 48, t_rows, jnp.where(lanes < 56, d_rows, place_rows))
        pack[8 * agg : 8 * agg + 8] = first
    half_way = SPAN * ngrp // 2
    packs[REACH * ngrp + grp] = pack[...]
    gather(pack, packs, pack_send, pack_recv, 1, half_way)

    for e in range(ELEMS):
        for k in range(6):
            t = table[e, k]
            here = (t >= ELEMS) & (t < 2 * ELEMS)
            near[e, k] = jnp.where(here, t - ELEMS, ELEMS)
    for side in range(2):
        chosen = [jnp.int32(0) for _ in range(HALO)]
        count = jnp.int32(0)
        for e in range(ELEMS):
            t = table[e, side]
            rank = jnp.int32(0)
            for other in range(ELEMS):
                u = table[other, side]
                lower = (u >= 0) & (u < t) if side == 0 else (u >= 2 * ELEMS) & (u < t)
                rank += lower.astype(jnp.int32)
            named = (t >= 0) & (t < ELEMS) if side == 0 else t >= 2 * ELEMS
            rank = jnp.minimum(rank, HALO - 1)
            far[e, side] = jnp.where(named, side * HALO + rank, 2 * HALO)
            chosen = [jnp.where(named & (rank == j), e, chosen[j]) for j in range(HALO)]
            count += named.astype(jnp.int32)
        for j in range(HALO):
            edge[side, j] = chosen[j]
        edge[side, HALO] = count
    window[ELEMS] = jnp.zeros((NODES, 3 * LOADS), BF16)
    window_m[ELEMS] = jnp.zeros((NODES, 3 * LOADS), BF16)
    halo[2 * HALO] = jnp.zeros((NODES, 3 * LOADS), BF16)
    halo_m[2 * HALO] = jnp.zeros((NODES, 3 * LOADS), BF16)

    loads[2].wait()
    for e in range(ELEMS):
        high, middle, low = three(exact(inverses[e], blocks[e]))
        da[e, 0:64] = high
        da[e, 64:128] = middle
        da[e, 128:192] = low

    def finish_step(k, copies, matrix, finish):
        arrive(copies)
        cut_halo(landed, k, halo)
        for e in range(ELEMS):
            finish(e, acc[e] + halo_part(matrix, e, halo))

    def local_step(matrix, source):
        cut(source, window)
        for e in range(ELEMS):
            acc[e] = local_part(matrix, e, window)

    def next_m(k, source, target):
        arrive(copies_m[k])
        cut(source, window_m)
        cut_halo_m(k)
        for e in range(ELEMS):
            target[e] = local_part(da, e, window_m) + halo_part(da, e, halo_m)

    def pre_finish(i):
        def finish(e, value):
            q = update[e] - value
            update[e] = q
            if i < 3:
                d = KEEP[i] * direction[e] + TAKE[i] * q
                direction[e] = d
                answer[e] = answer[e] + d
            else:
                field[e] = answer[e] + OMEGA * q

        return finish

    local_step(da, direction)
    for e in range(ELEMS):
        high, middle, low = three(blocks[e])
        a[e, 0:64] = high
        a[e, 64:128] = middle
        a[e, 128:192] = low
    for side in range(2):
        column = slice(64 + 64 * side, 128 + 64 * side)
        pieces = []
        for j in range(HALO):
            e = edge[side, j]
            rows = exact(prolong_t[e], blocks[e, :, column])
            pieces.append(jnp.where(edge[side, HALO] > j, rows, 0.0))
        strip_sent[0, side] = jnp.concatenate(pieces, axis=1)
    strip_copies = both(0, strip_sent, strip_landed, strip_send, strip_recv)
    finish_step(0, copies, da, pre_finish(1))

    copies = exchange(1, direction)
    next_m(0, prolong, m_one)
    copies_m.append(exchange_m(1, m_one))
    gather(pack, packs, pack_send, pack_recv, half_way, SPAN * ngrp)
    local_step(da, direction)

    finish_step(1, copies, da, pre_finish(2))

    copies = exchange(2, direction)
    next_m(1, m_one, m_two)
    copies_m.append(exchange_m(2, m_two))
    local_step(da, direction)

    wait_bytes(packs, gathered, pack_recv)
    wait_bytes(packs, gathered, pack_send)
    for ref in (kmat, amat, cmat, dmat):
        ref[...] = jnp.zeros((full, full), F32)

    def spread(rows, first, count, move):
        lane = iota(rows.shape, 1)
        rows = jnp.where((lane >= first) & (lane < first + count), rows, 0.0)
        rows = jnp.concatenate([rows, jnp.zeros((rows.shape[0], full - 128), F32)], axis=1)
        return pltpu.roll(rows, (move - first) % full, 1)

    for w in range(SPAN * ngrp):
        one = packs[w]
        amat[16 * w : 16 * w + 16, :] = spread(one, 0, 48, 16 * (w - 1))
        for agg in range(2):
            at = 16 * w + 8 * agg
            dmat[at : at + 8, :] = spread(one[8 * agg : 8 * agg + 8], 48, 8, at)
    tall = packs[...].reshape(wide, 128)
    tall = jnp.where(iota((wide, 128), 1) < 48, tall, 0.0)
    tall = exact(dmat[...], jnp.concatenate([tall, jnp.zeros((full - wide, 128), F32)], axis=0))
    for w in range(SPAN * ngrp):
        kmat[16 * w : 16 * w + 16, :] = spread(tall[16 * w : 16 * w + 16], 0, 48, 16 * (w - 1))
    size = 16 * ngrp
    for s in range(SPAN):
        stacked = jnp.concatenate([packs[s * ngrp + j] for j in range(ngrp)], axis=0)
        coarse = stacked[:, 64:128]
        target = 8.0 * stacked[:, 56:57] + (iota((size, 64), 0) % 8).astype(F32)
        places = jnp.where(jnp.abs(iota((size, 64), 1).astype(F32) - target) < 0.5, 1.0, 0.0)
        block = lax.dot_general(
            coarse, places, (((1,), (1,)), ((), ())), preferred_element_type=F32, precision=HIGHEST
        )
        row = jnp.concatenate([block, jnp.zeros((size, full - size), F32)], axis=1)
        cmat[size * s : size * s + size, :] = pltpu.roll(row, size * s, 1) if s else row
    finish_step(2, copies, da, pre_finish(3))

    arrive(strip_copies)
    for side in range(2):
        edge_rows = jnp.concatenate([field[give[side, j]] for j in range(HALO)], axis=0)
        share_sent[0, side] = exact(strip_landed[0, side], edge_rows)
    share_copies = both(0, share_sent, share_landed, share_send, share_recv)
    copies = exchange(3, update)
    cut(field, window)
    mine_b = jnp.zeros((16, LOADS), F32)
    for e in range(ELEMS):
        acc[e] = rhs[e].astype(F32) - local_part(a, e, window)
    for e in range(ELEMS):
        mine_b = mine_b + exact(prolong_t[e], acc[e])
    def smooth(rows):
        q = rows
        d = rows * TAKE[0]
        y = d
        for i in (1, 2):
            q = q - exact(d, kmat[...])
            d = KEEP[i] * d + TAKE[i] * q
            y = y + d
        return y

    shape = strip.shape
    start = (REACH * ngrp + grp - SIDE - 1) * 16
    unit = (iota(shape, 1) == iota(shape, 0) + start).astype(F32)
    u = smooth(unit)
    v = exact(u, kmat[...])
    strip[...] = v
    left[...] = 2.0 * u

    next_m(2, m_two, m_three)
    arrive(share_copies)
    own_b[...] = mine_b - (share_landed[0, 0] + share_landed[0, 1])
    gather(own_b, all_b, b_send, b_recv, 1, SPAN * ngrp)
    all_b[REACH * ngrp + grp] = own_b[...]

    def post_first(e, value):
        q0 = update[e]
        d0 = TAKE[0] * q0
        q1 = q0 - TAKE[0] * value
        d1 = KEEP[1] * d0 + TAKE[1] * q1
        update[e] = q1
        direction[e] = d1
        answer[e] = answer[e] + d0 + d1

    local_step(da, update)
    finish_step(3, copies, da, post_first)
    copies = exchange(4, direction)

    for e in range(ELEMS):
        one, two = m_one[e], m_two[e]
        g = one - OMEGA * two
        h = g - TAKE[0] * (two - OMEGA * m_three[e])
        step = KEEP[1] * TAKE[0] * g + TAKE[1] * h
        whole = (prolong[e] - OMEGA * one) - TAKE[0] * g - step
        m_one[e] = step
        m_two[e] = h
        m_three[e] = whole
    copies_m.append(exchange_m(3, m_one))

    m = exact(unit - strip[...], cmat[...])
    y = smooth(strip[...] + exact(m, amat[...]))
    strip[...] = m + exact(left[...] - y, dmat[...])

    arrive(copies_m[3])
    reach = 16 * (2 * SIDE + 1)
    rest = jnp.zeros((LOADS - reach, HALO * NODES), F32)
    for side in range(2):
        tall = jnp.concatenate([m_landed[3, side, 0:reach], rest], axis=0).T
        for j in range(HALO):
            field[side * HALO + j] = tall[NODES * j : NODES * j + NODES]

    wait_bytes(all_b, gathered, b_recv)
    values = all_b[...].reshape(wide, LOADS)
    padded = jnp.concatenate([values, jnp.zeros((full - wide, LOADS), F32)], axis=0)
    c = exact(strip[...], padded)
    rest = jnp.zeros((LOADS - reach, LOADS), F32)
    c_before, c_own, c_after = (
        jnp.concatenate([c[16 * i : 16 * i + reach], rest], axis=0) for i in range(3)
    )
    rows = ELEMS * NODES
    change = exact(m_one[...].reshape(rows, LOADS), c_own).reshape(ELEMS, NODES, LOADS)
    direction[...] = direction[...] - change

    arrive(copies)
    for side, c_side in enumerate((c_before, c_after)):
        some = field[side * HALO : side * HALO + HALO].reshape(HALO * NODES, LOADS)
        change = exact(some, c_side).reshape(HALO, NODES, LOADS)
        for j in range(HALO):
            store_pieces(halo, side * HALO + j, landed[4, side, j] - change[j])
    change = exact(m_two[...].reshape(rows, LOADS), c_own).reshape(ELEMS, NODES, LOADS)
    update[...] = update[...] - change
    change = exact(m_three[...].reshape(rows, LOADS), c_own).reshape(ELEMS, NODES, LOADS)
    answer[...] = answer[...] + change
    cut(direction, window)
    for e in range(ELEMS):
        q = update[e] - (local_part(da, e, window) + halo_part(da, e, halo))
        answer[e] = answer[e] + (KEEP[2] * direction[e] + TAKE[2] * q)

    copies = exchange(5, answer)
    wait_bytes(all_b, gathered, b_send)
    local_step(a, answer)
    sums = [jnp.zeros((8, LOADS), F32), jnp.zeros((8, LOADS), F32)]
    for e in range(ELEMS):
        x = answer[e]
        x_out[e] = x
        sums[0] = sums[0] + jnp.sum((rhs[e].astype(F32) * x).reshape(8, 8, LOADS), axis=0)

    def last(e, value):
        applied_out[e] = value
        sums[1] = sums[1] + jnp.sum((answer[e] * value).reshape(8, 8, LOADS), axis=0)

    finish_step(5, copies, a, last)
    row = iota((8, LOADS), 0)
    numerator = jnp.sum(sums[0], axis=0, keepdims=True)
    denominator = jnp.sum(sums[1], axis=0, keepdims=True)
    part[...] = jnp.where(row == 0, numerator, jnp.where(row == 1, denominator, 0.0))

    def combine(source, target, partner, rank, count, which):
        def body(i, carry):
            pltpu.make_async_remote_copy(
                src_ref=source,
                dst_ref=target.at[rank],
                send_sem=sum_send.at[which],
                recv_sem=sum_recv.at[which],
                device_id=partner(i),
                device_id_type=MESH,
            ).start()
            return carry

        lax.fori_loop(1, count, body, 0)
        target[rank] = source[...]
        wait_bytes(target, count - 1, sum_recv.at[which])
        return jnp.sum(target[...], axis=0)

    total[...] = combine(part, parts_near, near_partner, near_rank, near_count, 0)
    whole = combine(total, parts_far, far_partner, gy, ngy, 1)
    step_out[...] = jnp.broadcast_to(whole[0:1] / whole[1:2], (8, LOADS))
    wait_bytes(parts_near, near_count - 1, sum_send.at[0])
    wait_bytes(parts_far, ngy - 1, sum_send.at[1])
    for copy in pending:
        copy.wait_send()


def on_device(
    sizes,
    rhs,
    element_blocks,
    element_table,
    element_block_inverses,
    basis,
    element_aggregate,
    aggregate_blocks,
    aggregate_table,
    aggregate_inverse,
    coarse_map,
    coarse_owner,
    coarse_inverse,
):
    ngx, ngy, ngrp = sizes
    held = SPAN * ngrp
    full = -(-held * 16 // 128) * 128
    smem = pl.BlockSpec(memory_space=pltpu.SMEM)
    vmem = pl.BlockSpec(memory_space=pltpu.VMEM)
    hbm = pl.BlockSpec(memory_space=pltpu.HBM)
    shape = (ELEMS, NODES, LOADS)
    exchanges = 6
    cut_shape = (ELEMS + 1, NODES, 3 * LOADS)
    scratch = [
        pltpu.VMEM(shape, BF16),
        pltpu.VMEM((ELEMS, NODES, NODES), F32),
        pltpu.VMEM((ELEMS, NODES, 7 * NODES), F32),
        pltpu.VMEM((ELEMS, MODES, NODES), F32),
        pltpu.SMEM((ELEMS, 6), jnp.int32),
        pltpu.SMEM((ELEMS, 2), jnp.int32),
        pltpu.SMEM((2, HALO), jnp.int32),
        pltpu.SMEM((2, HALO + 1), jnp.int32),
        pltpu.VMEM((ELEMS, 192, 448), BF16),
        pltpu.VMEM((ELEMS, 192, 448), BF16),
        *([pltpu.VMEM(cut_shape, BF16)] * 4),
        *([pltpu.VMEM(shape, F32)] * 5),
        *([pltpu.VMEM((exchanges, 2, HALO, NODES, LOADS), F32)] * 2),
        pltpu.VMEM(shape, F32),
        pltpu.VMEM((ELEMS, 16, NODES), F32),
        *([pltpu.VMEM(shape, F32)] * 3),
        *([pltpu.VMEM((4, 2, 16 * (2 * SIDE + 1), HALO * NODES), F32)] * 2),
        *([pltpu.VMEM((1, 2, 16, HALO * NODES), F32)] * 2),
        *([pltpu.VMEM((1, 2, 16, LOADS), F32)] * 2),
        pltpu.VMEM((16, LOADS), F32),
        pltpu.VMEM((held, 16, LOADS), F32),
        *([pltpu.VMEM((full, full), F32)] * 4),
        *([pltpu.VMEM((16 * (2 * SIDE + 3), full), F32)] * 2),
        pltpu.VMEM((16, LOADS), F32),
        pltpu.VMEM((held, 16, LOADS), F32),
        pltpu.VMEM((8, LOADS), F32),
        pltpu.VMEM((ngx * ngrp, 8, LOADS), F32),
        pltpu.VMEM((8, LOADS), F32),
        pltpu.VMEM((ngy, 8, LOADS), F32),
        pltpu.SemaphoreType.DMA((4,)),
        *([pltpu.SemaphoreType.DMA((exchanges, 2))] * 2),
        *([pltpu.SemaphoreType.DMA((4, 2))] * 2),
        *([pltpu.SemaphoreType.DMA((1, 2))] * 4),
        *([pltpu.SemaphoreType.DMA] * 4),
        *([pltpu.SemaphoreType.DMA((2,))] * 2),
    ]
    x, applied, step = pl.pallas_call(
        functools.partial(kernel, sizes),
        out_shape=(
            jax.ShapeDtypeStruct(shape, F32),
            jax.ShapeDtypeStruct(shape, F32),
            jax.ShapeDtypeStruct((8, LOADS), F32),
        ),
        in_specs=[smem] * 5 + [hbm] * 4 + [vmem] * 3,
        out_specs=(vmem, vmem, vmem),
        scratch_shapes=scratch,
        compiler_params=pltpu.CompilerParams(
            collective_id=0, has_side_effects=True, vmem_limit_bytes=48 * 1024 * 1024
        ),
    )(
        element_table,
        element_aggregate,
        aggregate_table,
        coarse_map,
        coarse_owner,
        rhs,
        element_block_inverses,
        element_blocks,
        jnp.swapaxes(basis, 1, 2),
        aggregate_blocks,
        aggregate_inverse,
        coarse_inverse.reshape(8, 8, 64),
    )
    step = step[0:1][None]
    return step * x, rhs.astype(F32) - step * applied


def solution(mesh):
    sizes = tuple(mesh.shape[name] for name in ("gx", "gy", "grp"))
    slabs = P(("gx", "gy", "grp"), None, None)
    pairs = P(("gx", "gy", "grp"), None)
    ids = P(("gx", "gy", "grp"))
    return jax.shard_map(
        functools.partial(on_device, sizes),
        mesh=mesh,
        in_specs=(
            slabs,
            slabs,
            pairs,
            slabs,
            slabs,
            ids,
            slabs,
            pairs,
            slabs,
            ids,
            P(("gx", "gy"), None),
            P(("gx", "gy"), None, None),
        ),
        out_specs=(slabs, slabs),
        check_vma=False,
    )
```

```python
import functools

import jax
import jax.numpy as jnp
from jax import lax
from jax.experimental import pallas as pl
from jax.experimental.pallas import tpu as pltpu
from jax.sharding import PartitionSpec as P

OMEGA = 0.7
LOW_BOUND = 0.25
UPPER_LIMIT = 1.9
THETA = (UPPER_LIMIT + LOW_BOUND) / 2.0
DELTA = (UPPER_LIMIT - LOW_BOUND) / 2.0
SIGMA = THETA / DELTA
RHO = [1.0 / SIGMA]
for _ in range(2):
    RHO.append(1.0 / (2.0 * SIGMA - RHO[-1]))
KEEP = [0.0, RHO[1] * RHO[0], RHO[2] * RHO[1]]
TAKE = [1.0 / THETA, 2.0 * RHO[1] / DELTA, 2.0 * RHO[2] / DELTA]

ELEMS = 8
NODES = 64
MODES = 8
SIDE = 3
LOADS = 128
HALO = 4
REACH = 3
SPAN = 2 * REACH + 1
MESH = pl.DeviceIdType.MESH
HIGHEST = lax.Precision.HIGHEST
F32 = jnp.float32
BF16 = jnp.bfloat16


def dot(a, b):
    return jnp.dot(a, b, preferred_element_type=F32)


def exact(a, b):
    return jnp.dot(a, b, preferred_element_type=F32, precision=HIGHEST)


def three(v):
    high = v.astype(BF16)
    rest = v - high.astype(F32)
    middle = rest.astype(BF16)
    low = (rest - middle.astype(F32)).astype(BF16)
    return high, middle, low


def iota(shape, dim):
    return lax.broadcasted_iota(jnp.int32, shape, dim)


def kernel(
    sizes,
    table,
    member,
    coarse_table,
    coarse_map,
    owner,
    rhs_hbm,
    inverses_hbm,
    blocks_hbm,
    basis_hbm,
    coarse_blocks,
    coarse_inverses,
    group_inverse,
    x_out,
    applied_out,
    step_out,
    rhs,
    inverses,
    blocks,
    basis,
    near,
    far,
    give,
    edge,
    da,
    a,
    window,
    halo,
    window_m,
    halo_m,
    update,
    direction,
    answer,
    acc,
    field,
    sent,
    landed,
    prolong,
    prolong_t,
    m_one,
    m_two,
    m_three,
    m_sent,
    m_landed,
    strip_sent,
    strip_landed,
    share_sent,
    share_landed,
    pack,
    packs,
    kmat,
    amat,
    cmat,
    dmat,
    left,
    strip,
    own_b,
    all_b,
    part,
    parts_near,
    total,
    parts_far,
    load_sem,
    send_sem,
    recv_sem,
    m_send,
    m_recv,
    strip_send,
    strip_recv,
    share_send,
    share_recv,
    pack_send,
    pack_recv,
    b_send,
    b_recv,
    sum_send,
    sum_recv,
):
    ngx, ngy, ngrp = sizes
    groups = ngx * ngy
    devices = groups * ngrp
    wide = SPAN * ngrp * 16
    full = kmat.shape[0]
    rem, div = lax.rem, lax.div
    gx, gy, grp = (lax.axis_index(name) for name in ("gx", "gy", "grp"))
    group = gx * ngy + gy
    me = group * ngrp + grp

    def place(index):
        return (div(index, ngy * ngrp), rem(div(index, ngrp), ngy), rem(index, ngrp))

    before = place(rem(me + devices - 1, devices))
    after = place(rem(me + 1, devices))

    def gather_partner(i):
        turn = div(i, ngrp)
        half = div(turn + 1, 2)
        offset = half * (1 - 2 * rem(turn, 2))
        to_group = rem(group + offset + groups, groups)
        slot = (REACH - offset) * ngrp + grp
        return (div(to_group, ngy), rem(to_group, ngy), rem(grp + i, ngrp)), slot

    near_count = ngx * ngrp
    near_rank = gx * ngrp + grp

    def near_partner(i):
        rank = rem(near_rank + rem(near_count // 2 - 2 + i, near_count - 1) + 1, near_count)
        return (div(rank, ngrp), gy, rem(rank, ngrp))

    def far_partner(i):
        half = div(i, 2)
        return (gx, rem(gy + ngy // 2 + half * (2 * rem(i, 2) - 1) + ngy, ngy), grp)

    barrier = pltpu.get_barrier_semaphore()

    def greet(partner, count):
        def body(i, carry):
            pl.semaphore_signal(barrier, inc=1, device_id=partner(i), device_id_type=MESH)
            return carry

        lax.fori_loop(1, count, body, 0, unroll=True)

    greet(lambda i: gather_partner(i)[0], SPAN * ngrp)

    loads = []
    for i, (source, target) in enumerate(
        ((rhs_hbm, rhs), (inverses_hbm, inverses), (blocks_hbm, blocks), (basis_hbm, basis))
    ):
        copy = pltpu.make_async_copy(source, target, load_sem.at[i])
        copy.start()
        loads.append(copy)
    greet(near_partner, near_count)
    greet(far_partner, ngy)
    greetings = (SPAN * ngrp - 1) + (near_count - 1) + (ngy - 1)

    for side in range(2):
        chosen = [jnp.int32(0) for _ in range(HALO)]
        count = jnp.int32(0)
        for e in range(ELEMS):
            t = table[e, side]
            flag = (t >= 0) & (t < ELEMS) if side == 0 else t >= 2 * ELEMS
            chosen = [jnp.where(flag & (count == j), e, chosen[j]) for j in range(HALO)]
            count += flag.astype(jnp.int32)
        for j in range(HALO):
            give[side, j] = chosen[j]

    loads[0].wait()
    loads[1].wait()
    for e in range(ELEMS):
        pieces = jnp.concatenate(three(inverses[e]), axis=0)
        o = dot(pieces, rhs[e])
        q = o[0:64] + (o[64:128] + o[128:192])
        update[e] = q
        d = q * TAKE[0]
        direction[e] = d
        answer[e] = d

    pl.semaphore_wait(barrier, greetings)

    def ring(source, target, send, recv, side):
        return pltpu.make_async_remote_copy(
            src_ref=source,
            dst_ref=target,
            send_sem=send,
            recv_sem=recv,
            device_id=before if side == 0 else after,
            device_id_type=MESH,
        )

    pending = []

    def both(k, source, target, send, recv):
        copies = [ring(source.at[k, s], target.at[k, 1 - s], send.at[k, s], recv.at[k, s], s) for s in range(2)]
        for copy in copies:
            copy.start()
        pending.extend(copies)
        return copies

    def arrive(copies):
        for copy in copies:
            copy.wait_recv()

    def exchange(k, source):
        for side in range(2):
            for j in range(HALO):
                sent[k, side, j] = source[give[side, j]]
        return both(k, sent, landed, send_sem, recv_sem)

    def exchange_m(k, source):
        low, count = 16 * (SIDE - k), 16 * (2 * k + 1)
        copies = []
        for side in range(2):
            tall = jnp.concatenate([source[give[side, j]] for j in range(HALO)], axis=0)
            m_sent[k, side, 0:count] = tall.T[low : low + count]
            rows = pl.ds(0, count)
            copy = ring(
                m_sent.at[k, side, rows], m_landed.at[k, 1 - side, rows], m_send.at[k, side], m_recv.at[k, side], side
            )
            copy.start()
            copies.append(copy)
        pending.extend(copies)
        return copies

    def cut_halo_m(k):
        low, count = 16 * (SIDE - k), 16 * (2 * k + 1)
        for side in range(2):
            first = low - 16 if side == 0 else low + 16
            rows = [m_landed[k, side, 0:count], jnp.zeros((LOADS - first - count, HALO * NODES), F32)]
            if first:
                rows = [jnp.zeros((first, HALO * NODES), F32)] + rows
            tall = jnp.concatenate(rows, axis=0).T
            for j in range(HALO):
                store_pieces(halo_m, side * HALO + j, tall[NODES * j : NODES * j + NODES])

    def store_pieces(ref, slot, value):
        high, middle, low = three(value)
        ref[slot, :, 0:128] = high
        ref[slot, :, 128:256] = middle
        ref[slot, :, 256:384] = low

    def cut(source, into):
        for e in range(ELEMS):
            store_pieces(into, e, source[e])

    def cut_halo(source, k, into):
        for side in range(2):
            for j in range(HALO):
                store_pieces(into, side * HALO + j, source[k, side, j])

    def products(matrix, stack):
        o = dot(matrix, stack[:, 0:256])
        p = dot(matrix[0:64], stack[:, 256:384])
        small = o[64:128, 128:256] + o[128:192, 0:128] + p
        return o[0:64, 0:128] + ((o[0:64, 128:256] + o[64:128, 0:128]) + small)

    def local_part(matrix, e, of):
        stack = jnp.concatenate([of[e]] + [of[near[e, k]] for k in range(6)], axis=0)
        return products(matrix[e], stack)

    def halo_part(matrix, e, of):
        stack = jnp.concatenate([of[far[e, 0]], of[far[e, 1]]], axis=0)
        return products(matrix[e, :, 64:192], stack)

    def gather(source, target, send, recv, first, stop):

        def body(i, carry):
            device, slot = gather_partner(SPAN * ngrp - i)
            pltpu.make_async_remote_copy(
                src_ref=source,
                dst_ref=target.at[slot],
                send_sem=send,
                recv_sem=recv,
                device_id=device,
                device_id_type=MESH,
            ).start()
            return carry

        lax.fori_loop(first, stop, body, 0)

    def wait_bytes(target, count, sem):
        pltpu.make_async_copy(target.at[pl.ds(0, count)], target.at[pl.ds(0, count)], sem).wait()

    gathered = SPAN * ngrp - 1

    copies = exchange(0, direction)

    loads[3].wait()
    first_lane = 16 * SIDE
    for e in range(ELEMS):
        spot = iota((16, MODES), 0) == iota((16, MODES), 1) + MODES * member[e]
        rows = exact(spot.astype(F32), basis[e])
        prolong_t[e] = rows
        tall = jnp.concatenate(
            [jnp.zeros((first_lane, NODES), F32), rows, jnp.zeros((112 - first_lane, NODES), F32)], axis=0
        )
        prolong[e] = tall.T
    copies_m = [exchange_m(0, prolong)]

    lanes = iota((8, 128), 1)
    for agg in range(2):
        row = iota((56, 128), 0)
        want = jnp.full((56, 128), 2 + agg, jnp.int32)
        for k in range(6):
            want = jnp.where(row // 8 == k + 1, coarse_table[agg, k], want)
        spot = iota((56, 128), 1) == want * 8 + row % 8
        t_rows = exact(coarse_blocks[agg], spot.astype(F32))
        small = iota((8, 128), 1) == iota((8, 128), 0) + 48
        d_rows = exact(coarse_inverses[agg], small.astype(F32))
        whole = coarse_map[agg]
        coarse_rows = group_inverse[whole]
        mine = owner[0, whole]
        kept = jnp.zeros((8, 64), F32)
        for c in range(8):
            same = (owner[0, c] == mine).astype(F32)
            kept = jnp.where(iota((8, 64), 1) // 8 == c, same, kept)
        shift = iota((64, 128), 1) == iota((64, 128), 0) + 64
        m_rows = exact(jnp.where(kept > 0.5, coarse_rows, 0.0), shift.astype(F32))
        place_rows = jnp.where(lanes == 56, whole.astype(F32), m_rows)
        first = jnp.where(lanes < 48, t_rows, jnp.where(lanes < 56, d_rows, place_rows))
        pack[8 * agg : 8 * agg + 8] = first
    half_way = SPAN * ngrp // 2
    packs[REACH * ngrp + grp] = pack[...]
    gather(pack, packs, pack_send, pack_recv, 1, half_way)

    for e in range(ELEMS):
        for k in range(6):
            t = table[e, k]
            here = (t >= ELEMS) & (t < 2 * ELEMS)
            near[e, k] = jnp.where(here, t - ELEMS, ELEMS)
    for side in range(2):
        chosen = [jnp.int32(0) for _ in range(HALO)]
        count = jnp.int32(0)
        for e in range(ELEMS):
            t = table[e, side]
            rank = jnp.int32(0)
            for other in range(ELEMS):
                u = table[other, side]
                lower = (u >= 0) & (u < t) if side == 0 else (u >= 2 * ELEMS) & (u < t)
                rank += lower.astype(jnp.int32)
            named = (t >= 0) & (t < ELEMS) if side == 0 else t >= 2 * ELEMS
            rank = jnp.minimum(rank, HALO - 1)
            far[e, side] = jnp.where(named, side * HALO + rank, 2 * HALO)
            chosen = [jnp.where(named & (rank == j), e, chosen[j]) for j in range(HALO)]
            count += named.astype(jnp.int32)
        for j in range(HALO):
            edge[side, j] = chosen[j]
        edge[side, HALO] = count
    window[ELEMS] = jnp.zeros((NODES, 3 * LOADS), BF16)
    window_m[ELEMS] = jnp.zeros((NODES, 3 * LOADS), BF16)
    halo[2 * HALO] = jnp.zeros((NODES, 3 * LOADS), BF16)
    halo_m[2 * HALO] = jnp.zeros((NODES, 3 * LOADS), BF16)

    loads[2].wait()
    for e in range(ELEMS):
        high, middle, low = three(exact(inverses[e], blocks[e]))
        da[e, 0:64] = high
        da[e, 64:128] = middle
        da[e, 128:192] = low

    def finish_step(k, copies, matrix, finish):
        arrive(copies)
        cut_halo(landed, k, halo)
        for e in range(ELEMS):
            finish(e, acc[e] + halo_part(matrix, e, halo))

    def local_step(matrix, source):
        cut(source, window)
        for e in range(ELEMS):
            acc[e] = local_part(matrix, e, window)

    def next_m(k, source, target):
        arrive(copies_m[k])
        cut(source, window_m)
        cut_halo_m(k)
        for e in range(ELEMS):
            target[e] = local_part(da, e, window_m) + halo_part(da, e, halo_m)

    def pre_finish(i):
        def finish(e, value):
            q = update[e] - value
            update[e] = q
            if i < 3:
                d = KEEP[i] * direction[e] + TAKE[i] * q
                direction[e] = d
                answer[e] = answer[e] + d
            else:
                field[e] = answer[e] + OMEGA * q

        return finish

    local_step(da, direction)
    for e in range(ELEMS):
        high, middle, low = three(blocks[e])
        a[e, 0:64] = high
        a[e, 64:128] = middle
        a[e, 128:192] = low
    for side in range(2):
        column = slice(64 + 64 * side, 128 + 64 * side)
        pieces = []
        for j in range(HALO):
            e = edge[side, j]
            rows = exact(prolong_t[e], blocks[e, :, column])
            pieces.append(jnp.where(edge[side, HALO] > j, rows, 0.0))
        strip_sent[0, side] = jnp.concatenate(pieces, axis=1)
    strip_copies = both(0, strip_sent, strip_landed, strip_send, strip_recv)
    finish_step(0, copies, da, pre_finish(1))

    copies = exchange(1, direction)
    next_m(0, prolong, m_one)
    copies_m.append(exchange_m(1, m_one))
    gather(pack, packs, pack_send, pack_recv, half_way, SPAN * ngrp)
    local_step(da, direction)

    finish_step(1, copies, da, pre_finish(2))

    copies = exchange(2, direction)
    next_m(1, m_one, m_two)
    copies_m.append(exchange_m(2, m_two))
    local_step(da, direction)

    wait_bytes(packs, gathered, pack_recv)
    wait_bytes(packs, gathered, pack_send)
    for ref in (kmat, amat, cmat, dmat):
        ref[...] = jnp.zeros((full, full), F32)

    def spread(rows, first, count, move):
        lane = iota(rows.shape, 1)
        rows = jnp.where((lane >= first) & (lane < first + count), rows, 0.0)
        rows = jnp.concatenate([rows, jnp.zeros((rows.shape[0], full - 128), F32)], axis=1)
        return pltpu.roll(rows, (move - first) % full, 1)

    for w in range(SPAN * ngrp):
        one = packs[w]
        amat[16 * w : 16 * w + 16, :] = spread(one, 0, 48, 16 * (w - 1))
        for agg in range(2):
            at = 16 * w + 8 * agg
            dmat[at : at + 8, :] = spread(one[8 * agg : 8 * agg + 8], 48, 8, at)
    tall = packs[...].reshape(wide, 128)
    tall = jnp.where(iota((wide, 128), 1) < 48, tall, 0.0)
    tall = exact(dmat[...], jnp.concatenate([tall, jnp.zeros((full - wide, 128), F32)], axis=0))
    for w in range(SPAN * ngrp):
        kmat[16 * w : 16 * w + 16, :] = spread(tall[16 * w : 16 * w + 16], 0, 48, 16 * (w - 1))
    size = 16 * ngrp
    for s in range(SPAN):
        stacked = jnp.concatenate([packs[s * ngrp + j] for j in range(ngrp)], axis=0)
        coarse = stacked[:, 64:128]
        target = 8.0 * stacked[:, 56:57] + (iota((size, 64), 0) % 8).astype(F32)
        places = jnp.where(jnp.abs(iota((size, 64), 1).astype(F32) - target) < 0.5, 1.0, 0.0)
        block = lax.dot_general(
            coarse, places, (((1,), (1,)), ((), ())), preferred_element_type=F32, precision=HIGHEST
        )
        row = jnp.concatenate([block, jnp.zeros((size, full - size), F32)], axis=1)
        cmat[size * s : size * s + size, :] = pltpu.roll(row, size * s, 1) if s else row
    finish_step(2, copies, da, pre_finish(3))

    arrive(strip_copies)
    for side in range(2):
        edge_rows = jnp.concatenate([field[give[side, j]] for j in range(HALO)], axis=0)
        share_sent[0, side] = exact(strip_landed[0, side], edge_rows)
    share_copies = both(0, share_sent, share_landed, share_send, share_recv)
    copies = exchange(3, update)
    cut(field, window)
    mine_b = jnp.zeros((16, LOADS), F32)
    for e in range(ELEMS):
        acc[e] = rhs[e].astype(F32) - local_part(a, e, window)
    for e in range(ELEMS):
        mine_b = mine_b + exact(prolong_t[e], acc[e])
    def smooth(rows):
        q = rows
        d = rows * TAKE[0]
        y = d
        for i in (1, 2):
            q = q - exact(d, kmat[...])
            d = KEEP[i] * d + TAKE[i] * q
            y = y + d
        return y

    shape = strip.shape
    start = (REACH * ngrp + grp - SIDE - 1) * 16
    unit = (iota(shape, 1) == iota(shape, 0) + start).astype(F32)
    u = smooth(unit)
    v = exact(u, kmat[...])
    strip[...] = v
    left[...] = 2.0 * u

    next_m(2, m_two, m_three)
    arrive(share_copies)
    own_b[...] = mine_b - (share_landed[0, 0] + share_landed[0, 1])
    gather(own_b, all_b, b_send, b_recv, 1, SPAN * ngrp)
    all_b[REACH * ngrp + grp] = own_b[...]

    def post_first(e, value):
        q0 = update[e]
        d0 = TAKE[0] * q0
        q1 = q0 - TAKE[0] * value
        d1 = KEEP[1] * d0 + TAKE[1] * q1
        update[e] = q1
        direction[e] = d1
        answer[e] = answer[e] + d0 + d1

    local_step(da, update)
    finish_step(3, copies, da, post_first)
    copies = exchange(4, direction)

    for e in range(ELEMS):
        one, two = m_one[e], m_two[e]
        g = one - OMEGA * two
        h = g - TAKE[0] * (two - OMEGA * m_three[e])
        step = KEEP[1] * TAKE[0] * g + TAKE[1] * h
        whole = (prolong[e] - OMEGA * one) - TAKE[0] * g - step
        m_one[e] = step
        m_two[e] = h
        m_three[e] = whole
    copies_m.append(exchange_m(3, m_one))

    m = exact(unit - strip[...], cmat[...])
    y = smooth(strip[...] + exact(m, amat[...]))
    strip[...] = m + exact(left[...] - y, dmat[...])

    arrive(copies_m[3])
    reach = 16 * (2 * SIDE + 1)
    rest = jnp.zeros((LOADS - reach, HALO * NODES), F32)
    for side in range(2):
        tall = jnp.concatenate([m_landed[3, side, 0:reach], rest], axis=0).T
        for j in range(HALO):
            field[side * HALO + j] = tall[NODES * j : NODES * j + NODES]

    wait_bytes(all_b, gathered, b_recv)
    values = all_b[...].reshape(wide, LOADS)
    padded = jnp.concatenate([values, jnp.zeros((full - wide, LOADS), F32)], axis=0)
    c = exact(strip[...], padded)
    rest = jnp.zeros((LOADS - reach, LOADS), F32)
    c_before, c_own, c_after = (
        jnp.concatenate([c[16 * i : 16 * i + reach], rest], axis=0) for i in range(3)
    )
    rows = ELEMS * NODES
    change = exact(m_one[...].reshape(rows, LOADS), c_own).reshape(ELEMS, NODES, LOADS)
    direction[...] = direction[...] - change

    arrive(copies)
    for side, c_side in enumerate((c_before, c_after)):
        some = field[side * HALO : side * HALO + HALO].reshape(HALO * NODES, LOADS)
        change = exact(some, c_side).reshape(HALO, NODES, LOADS)
        for j in range(HALO):
            store_pieces(halo, side * HALO + j, landed[4, side, j] - change[j])
    change = exact(m_two[...].reshape(rows, LOADS), c_own).reshape(ELEMS, NODES, LOADS)
    update[...] = update[...] - change
    change = exact(m_three[...].reshape(rows, LOADS), c_own).reshape(ELEMS, NODES, LOADS)
    answer[...] = answer[...] + change
    cut(direction, window)
    for e in range(ELEMS):
        q = update[e] - (local_part(da, e, window) + halo_part(da, e, halo))
        answer[e] = answer[e] + (KEEP[2] * direction[e] + TAKE[2] * q)

    copies = exchange(5, answer)
    wait_bytes(all_b, gathered, b_send)
    local_step(a, answer)
    sums = [jnp.zeros((8, LOADS), F32), jnp.zeros((8, LOADS), F32)]
    for e in range(ELEMS):
        x = answer[e]
        x_out[e] = x
        sums[0] = sums[0] + jnp.sum((rhs[e].astype(F32) * x).reshape(8, 8, LOADS), axis=0)

    def last(e, value):
        applied_out[e] = value
        sums[1] = sums[1] + jnp.sum((answer[e] * value).reshape(8, 8, LOADS), axis=0)

    finish_step(5, copies, a, last)
    row = iota((8, LOADS), 0)
    numerator = jnp.sum(sums[0], axis=0, keepdims=True)
    denominator = jnp.sum(sums[1], axis=0, keepdims=True)
    part[...] = jnp.where(row == 0, numerator, jnp.where(row == 1, denominator, 0.0))

    def combine(source, target, partner, rank, count, which):
        def body(i, carry):
            pltpu.make_async_remote_copy(
                src_ref=source,
                dst_ref=target.at[rank],
                send_sem=sum_send.at[which],
                recv_sem=sum_recv.at[which],
                device_id=partner(i),
                device_id_type=MESH,
            ).start()
            return carry

        lax.fori_loop(1, count, body, 0)
        target[rank] = source[...]
        wait_bytes(target, count - 1, sum_recv.at[which])
        return jnp.sum(target[...], axis=0)

    total[...] = combine(part, parts_near, near_partner, near_rank, near_count, 0)
    whole = combine(total, parts_far, far_partner, gy, ngy, 1)
    step_out[...] = jnp.broadcast_to(whole[0:1] / whole[1:2], (8, LOADS))
    wait_bytes(parts_near, near_count - 1, sum_send.at[0])
    wait_bytes(parts_far, ngy - 1, sum_send.at[1])
    for copy in pending:
        copy.wait_send()


def on_device(
    sizes,
    rhs,
    element_blocks,
    element_table,
    element_block_inverses,
    basis,
    element_aggregate,
    aggregate_blocks,
    aggregate_table,
    aggregate_inverse,
    coarse_map,
    coarse_owner,
    coarse_inverse,
):
    ngx, ngy, ngrp = sizes
    held = SPAN * ngrp
    full = -(-held * 16 // 128) * 128
    smem = pl.BlockSpec(memory_space=pltpu.SMEM)
    vmem = pl.BlockSpec(memory_space=pltpu.VMEM)
    hbm = pl.BlockSpec(memory_space=pltpu.HBM)
    shape = (ELEMS, NODES, LOADS)
    exchanges = 6
    cut_shape = (ELEMS + 1, NODES, 3 * LOADS)
    scratch = [
        pltpu.VMEM(shape, BF16),
        pltpu.VMEM((ELEMS, NODES, NODES), F32),
        pltpu.VMEM((ELEMS, NODES, 7 * NODES), F32),
        pltpu.VMEM((ELEMS, MODES, NODES), F32),
        pltpu.SMEM((ELEMS, 6), jnp.int32),
        pltpu.SMEM((ELEMS, 2), jnp.int32),
        pltpu.SMEM((2, HALO), jnp.int32),
        pltpu.SMEM((2, HALO + 1), jnp.int32),
        pltpu.VMEM((ELEMS, 192, 448), BF16),
        pltpu.VMEM((ELEMS, 192, 448), BF16),
        *([pltpu.VMEM(cut_shape, BF16)] * 4),
        *([pltpu.VMEM(shape, F32)] * 5),
        *([pltpu.VMEM((exchanges, 2, HALO, NODES, LOADS), F32)] * 2),
        pltpu.VMEM(shape, F32),
        pltpu.VMEM((ELEMS, 16, NODES), F32),
        *([pltpu.VMEM(shape, F32)] * 3),
        *([pltpu.VMEM((4, 2, 16 * (2 * SIDE + 1), HALO * NODES), F32)] * 2),
        *([pltpu.VMEM((1, 2, 16, HALO * NODES), F32)] * 2),
        *([pltpu.VMEM((1, 2, 16, LOADS), F32)] * 2),
        pltpu.VMEM((16, LOADS), F32),
        pltpu.VMEM((held, 16, LOADS), F32),
        *([pltpu.VMEM((full, full), F32)] * 4),
        *([pltpu.VMEM((16 * (2 * SIDE + 3), full), F32)] * 2),
        pltpu.VMEM((16, LOADS), F32),
        pltpu.VMEM((held, 16, LOADS), F32),
        pltpu.VMEM((8, LOADS), F32),
        pltpu.VMEM((ngx * ngrp, 8, LOADS), F32),
        pltpu.VMEM((8, LOADS), F32),
        pltpu.VMEM((ngy, 8, LOADS), F32),
        pltpu.SemaphoreType.DMA((4,)),
        *([pltpu.SemaphoreType.DMA((exchanges, 2))] * 2),
        *([pltpu.SemaphoreType.DMA((4, 2))] * 2),
        *([pltpu.SemaphoreType.DMA((1, 2))] * 4),
        *([pltpu.SemaphoreType.DMA] * 4),
        *([pltpu.SemaphoreType.DMA((2,))] * 2),
    ]
    x, applied, step = pl.pallas_call(
        functools.partial(kernel, sizes),
        out_shape=(
            jax.ShapeDtypeStruct(shape, F32),
            jax.ShapeDtypeStruct(shape, F32),
            jax.ShapeDtypeStruct((8, LOADS), F32),
        ),
        in_specs=[smem] * 5 + [hbm] * 4 + [vmem] * 3,
        out_specs=(vmem, vmem, vmem),
        scratch_shapes=scratch,
        compiler_params=pltpu.CompilerParams(
            collective_id=0, has_side_effects=True, vmem_limit_bytes=64 * 1024 * 1024
        ),
    )(
        element_table,
        element_aggregate,
        aggregate_table,
        coarse_map,
        coarse_owner,
        rhs,
        element_block_inverses,
        element_blocks,
        jnp.swapaxes(basis, 1, 2),
        aggregate_blocks,
        aggregate_inverse,
        coarse_inverse.reshape(8, 8, 64),
    )
    step = step[0:1][None]
    return step * x, rhs.astype(F32) - step * applied


def solution(mesh):
    sizes = tuple(mesh.shape[name] for name in ("gx", "gy", "grp"))
    slabs = P(("gx", "gy", "grp"), None, None)
    pairs = P(("gx", "gy", "grp"), None)
    ids = P(("gx", "gy", "grp"))
    return jax.shard_map(
        functools.partial(on_device, sizes),
        mesh=mesh,
        in_specs=(
            slabs,
            slabs,
            pairs,
            slabs,
            slabs,
            ids,
            slabs,
            pairs,
            slabs,
            ids,
            P(("gx", "gy"), None),
            P(("gx", "gy"), None, None),
        ),
        out_specs=(slabs, slabs),
        check_vma=False,
    )
```
